512 devices in a mesh: rep: 32 (over z, core), shard: 16 (over y, x).
Axes of the slice: x: 4, y: 4, z: 16, core: 2. Of those that a mesh axis runs over, the one named last changes fastest.
Arguments:
- inputs: bfloat16 [32, 2048, 8192], P('rep', 'shard'), may hold values from -6 to 6
- target: bfloat16 [32, 2048, 512], P('rep', 'shard'), may hold values from -6 to 6
- weights: bfloat16 [32, 8192, 512], P('rep', 'shard'), may hold values from -0.0625 to 0.0625
- feedback: bfloat16 [32, 8192, 512], P('rep', 'shard'), may hold values from -6 to 6
- counts: int32 [32, 16], P('rep', 'shard'), may hold values from 16 to 128, as said below
- blocks: int32 [32, 16, 128], P('rep', 'shard'), may hold values from 0 to 2047, as said below
Outputs:
- outer_update: float32 [8192, 512], P('shard')
- new_feedback: bfloat16 [32, 8192, 512], P('rep', 'shard')
The draws below stay inside these ranges and needn't reach their ends.
Inputs may be any that keep to these rules, and one draw needn't show every extreme that they name: `counts`: in every shard index some replica keeps exactly 128 blocks. The 128 slots of one device hold distinct block numbers; only the first counts slots are kept; the others hold block numbers that this device does not keep (other replicas may keep them). All replicas of one shard index draw all their slots from a common set of 512 blocks.
All inputs are finite; a program needn't handle non-finite values.
Results may differ from the reference program's by a relative error of at most 0.0034.
Values may be sent and summed in bfloat16 or wider, within the bound.
A program may use at most 64 MiB of HBM per device.

```python
import jax
import jax.numpy as jnp
from jax import lax

D = 8192
KW = 512
TOK_DEV = 128
CAP = 128
BLOCK = 128
TOK_REP = 2048
NBLK = 2048
POOL = 512
N_REP = 32
N_SHARD = 16


def draw_counts(key, part):
    key = jax.random.fold_in(key, 11)
    key_base, key_full = jax.random.split(key)
    lowest = max(CAP // 8, 1)
    base = jax.random.randint(key_base, (N_REP, N_SHARD), lowest, CAP + 1)
    full_rep = jax.random.randint(key_full, (N_SHARD,), 0, N_REP)
    replica = jnp.arange(N_REP)[:, None]
    return jnp.where(replica == full_rep[None, :], CAP, base).astype(jnp.int32)


def draw_blocks(key, part):
    key = jax.random.fold_in(key, 23)

    def column(shard_id):
        common = jax.random.permutation(jax.random.fold_in(key, shard_id), NBLK)[:POOL]

        def single(rep_id):
            inner = jax.random.fold_in(jax.random.fold_in(key, shard_id + N_SHARD), rep_id)
            picked = jax.random.permutation(inner, POOL)[:CAP]
            return common[picked]
        return jax.vmap(single)(jnp.arange(N_REP))
    table = jax.vmap(column)(jnp.arange(N_SHARD))
    return jnp.transpose(table, (1, 0, 2)).astype(jnp.int32)


def block_levels(own_key, extent, shards, smallest, high):
    gain, own = 1.0, jax.random.fold_in(own_key, 6)
    for position, shards_of in shards:
        heights = jnp.exp(jax.random.uniform(jax.random.fold_in(own, position), (shards_of,), jnp.float32, smallest / len(shards), high / len(shards)))
        gain = gain * jnp.repeat(heights, extent[position] // shards_of).reshape([-1 if axis == position else 1 for axis in range(len(extent))])
    return gain


def noise(key, shape, deviation, limit, cuts=(), kind=jnp.bfloat16):
    entries = jax.random.normal(key, shape, jnp.float32) * deviation
    if len(cuts) > 0:
        entries = block_levels(key, shape, cuts, -0.22, 0.18) * entries
    return jnp.clip(entries, min=-limit, max=limit).astype(kind)


def setup_inputs(seed: int = 0) -> dict:
    key_list = jax.random.split(jax.random.key(seed), 7)
    inputs = noise(key_list[0], (N_REP, TOK_REP, D), 1.0, 6.0, ((0, 32), (1, 16)))
    target = noise(key_list[1], (N_REP, TOK_REP, KW), 1.0, 6.0, ((0, 32), (1, 16)))
    weights = noise(key_list[2], (N_REP, D, KW), D ** -0.5, 0.0625, ((0, 32), (1, 16)))
    feedback = noise(key_list[3], (N_REP, D, KW), 1.0, 6.0, ((0, 32), (1, 16)))
    counts = draw_counts(jax.random.fold_in(key_list[6], 71), 0)
    blocks = draw_blocks(jax.random.fold_in(key_list[6], 71), 0)
    return {"inputs": inputs, "target": target, "weights": weights, "feedback": feedback, "counts": counts, "blocks": blocks}


def replica_step(summed, items):
    inputs, target, weights, feedback, counts, blocks = items
    key_proj = jnp.dot(inputs, weights, preferred_element_type=jnp.float32)
    slopes = ((key_proj - target.astype(jnp.float32)) / TOK_DEV).astype(jnp.bfloat16)
    gradient = jnp.dot(inputs.T, slopes, preferred_element_type=jnp.float32)
    pseudo = gradient + feedback.astype(jnp.float32)
    blocked = pseudo.reshape(N_SHARD, NBLK, BLOCK)
    in_use = (jnp.arange(CAP, dtype=jnp.int32)[None, :] < counts[:, None]).astype(jnp.float32)
    shard_ids = jnp.broadcast_to(jnp.arange(N_SHARD, dtype=jnp.int32)[:, None], blocks.shape)
    kept_mask = jnp.zeros((N_SHARD, NBLK), jnp.float32).at[shard_ids, blocks].add(in_use)
    chosen = kept_mask[..., None] > 0
    kept = jnp.where(chosen, blocked, jnp.zeros_like(blocked))
    residue = jnp.where(chosen, jnp.zeros_like(blocked), blocked)
    summed = summed + kept.reshape(D, KW)
    return summed, residue.reshape(D, KW).astype(jnp.bfloat16)


def reference(inputs, target, weights, feedback, counts, blocks):
    start = jnp.zeros((D, KW), jnp.float32)
    summed, residues = lax.scan(replica_step, start, (inputs, target, weights, feedback, counts, blocks))
    return summed / N_REP, residues
```

```python
import jax
import jax.numpy as jnp
from jax import lax
from jax.experimental import pallas as pl
from jax.experimental.pallas import tpu as pltpu
from jax.sharding import PartitionSpec as P

MESH = pl.DeviceIdType.MESH
F32, BF16, I32 = jnp.float32, jnp.bfloat16, jnp.int32
UNUSED = 1 << 16
FAR_FIRST = (2, 1, 3)


def dot(a, b):
    return jnp.dot(a, b, preferred_element_type=F32)


def dot_nt(a, b):
    return lax.dot_general(a, b, (((1,), (1,)), ((), ())), preferred_element_type=F32)


def kernel(
    x_ref, tgt_ref, w_ref, fb_ref, cnt_ref, slot_ref,
    outer_ref, newfb_ref,
    xs, xt, wg, acc, kp_out, kp_in, slopes, g_own, g_out, g_in, k_out, k_in, k_own,
    meta, meta_b, meta_z, sel, expand, pool, kept, pool_val, pool_in, part16, rs_in, res,
    x_send, x_recv, w_send, w_recv, loc_sem, kp_send, kp_recv, sl_send, sl_recv,
    g_send, g_recv, k_send, k_recv, m_send, m_recv, mz_send, mz_recv,
    p_send, p_recv, rs_send, rs_recv, ag_send, ag_recv, q_send, q_recv,
):
    rep, shard = lax.axis_index("rep"), lax.axis_index("shard")
    core, z = lax.rem(rep, 2), rep // 2
    y, x = shard // 4, lax.rem(shard, 4)
    a = x * (1 - core) + y * core
    b = y * (1 - core) + x * core

    def shard_of(aa, bb):
        return (bb * (1 - core) + aa * core) * 4 + (aa * (1 - core) + bb * core)

    def along_a(k):
        return (rep, shard_of(lax.rem(a + k, 4), b))

    def along_b(k):
        return (rep, shard_of(a, lax.rem(b + k, 4)))

    def along_z(k):
        return (lax.rem(rep + 2 * k, 32), shard)

    twin = (rep + 1 - 2 * core, shard)

    def remote(src, dst, send, recv, device):
        return pltpu.make_async_remote_copy(
            src_ref=src, dst_ref=dst, send_sem=send, recv_sem=recv, device_id=device, device_id_type=MESH
        )

    barrier = pltpu.get_barrier_semaphore()
    for k in (1, 2, 3):
        pl.semaphore_signal(barrier, inc=1, device_id=along_a(k), device_id_type=MESH)
        pl.semaphore_signal(barrier, inc=1, device_id=along_b(k), device_id_type=MESH)
    pl.semaphore_signal(barrier, inc=1, device_id=twin, device_id_type=MESH)

    @pl.loop(1, 16)
    def _(k):
        pl.semaphore_signal(barrier, inc=1, device_id=along_z(k), device_id_type=MESH)

    in_use = lax.broadcasted_iota(I32, (8, 128), 1) < cnt_ref[0, 0]
    meta[0] = jnp.where(in_use, jnp.broadcast_to(slot_ref[...], (8, 128)), UNUSED)
    pl.semaphore_wait(barrier, 22)

    m_copies = [remote(meta.at[0], meta_b.at[4 - k], m_send.at[k], m_recv.at[4 - k], along_b(k)) for k in (1, 2, 3)]
    m_copies.append(remote(meta.at[0], meta.at[1], m_send.at[0], m_recv.at[0], twin))
    for copy in m_copies:
        copy.start()
    locals_ = [pltpu.make_async_copy(w_ref, wg.at[0], loc_sem.at[4])]
    for j in range(4):
        own = pl.multiple_of(shard_of(a, lax.rem(b + j, 4)) * 512, 512)
        locals_.append(pltpu.make_async_copy(x_ref.at[:, pl.ds(own, 512)], xs.at[j, pl.ds(0, 128)], loc_sem.at[j]))
    x_copies, w_copies = {}, {}
    for k in FAR_FIRST:
        w_copies[k] = remote(w_ref, wg.at[4 - k], w_send.at[k], w_recv.at[4 - k], along_b(k))
        w_copies[k].start()
    for j in (0, 1, 3, 2):
        for k in FAR_FIRST:
            cols = pl.multiple_of(shard_of(lax.rem(a + k, 4), lax.rem(b + j, 4)) * 512, 512)
            x_copies[j, k] = remote(
                x_ref.at[:, pl.ds(cols, 512)], xs.at[j, pl.ds((4 - k) * 128, 128)],
                x_send.at[j, k], x_recv.at[j, 4 - k], along_a(k),
            )
            x_copies[j, k].start()
    for copy in locals_:
        copy.start()

    m_copies[3].wait()
    row0 = lax.broadcasted_iota(I32, (8, 128), 0) == 0
    meta_z[0] = jnp.where(row0, meta[0], meta[1])

    @pl.loop(1, 16)
    def _(k):
        remote(meta_z.at[0], meta_z.at[16 - k], mz_send.at[k], mz_recv.at[16 - k], along_z(k)).start()

    rows512 = lax.broadcasted_iota(I32, (512, 128), 0)
    rows128 = lax.broadcasted_iota(I32, (128, 128), 0)
    lanes128 = lax.broadcasted_iota(I32, (128, 128), 1)
    own_list = meta[0, 0:1, :]
    own_rows = jnp.where(rows512 == (own_list >> 2), 1.0, 0.0).astype(BF16)
    for c in range(4):
        is_c = jnp.where((jnp.broadcast_to(own_list, (128, 128)) & 3) == c, 1.0, 0.0).astype(BF16)
        kept[:, c * 128:(c + 1) * 128] = dot_nt(own_rows, is_c).astype(BF16)
    for k in (1, 2, 3):
        m_copies[k - 1].wait()
    for j in range(4):
        lst = meta[0, 0:1, :] if j == 0 else meta_b[j, 0:1, :]
        turned = jnp.transpose(jnp.broadcast_to(lst, (128, 128)))
        key = (turned & 3) * 512 + (turned >> 2)
        for n in range(16):
            sel[j, :, n * 128:(n + 1) * 128] = jnp.where(key == lanes128 + n * 128, 1.0, 0.0).astype(BF16)

    @pl.loop(1, 16)
    def _(k):
        remote(meta_z.at[0], meta_z.at[16 - k], mz_send.at[k], mz_recv.at[16 - k], along_z(k)).wait_send()
        remote(meta_z.at[0], meta_z.at[k], mz_send.at[k], mz_recv.at[k], along_z(k)).wait_recv()

    def count(i, total):
        for r in range(2):
            lst = meta_z[i, r:r + 1, :]
            in_rows = jnp.where(rows512 == (lst >> 2), 1.0, 0.0).astype(BF16)
            in_cols = jnp.where(rows128 == (jnp.broadcast_to(lst, (128, 128)) & 3), 1.0, 0.0).astype(BF16)
            total = total + dot_nt(in_rows, in_cols)
        return total

    present = lax.fori_loop(0, 16, count, jnp.zeros((512, 128), F32)) > 0.5
    lower = jnp.where(
        lax.broadcasted_iota(I32, (512, 512), 0) >= lax.broadcasted_iota(I32, (512, 512), 1), 1.0, 0.0
    ).astype(BF16)
    upto = dot(lower, jnp.where(present, 1.0, 0.0).astype(BF16))
    totals = upto[511:512, :]
    lane = lax.broadcasted_iota(I32, (1, 128), 1)
    offset = jnp.zeros((1, 128), F32)
    for c in range(3):
        offset = offset + jnp.where(lane > c, totals[:, c:c + 1], 0.0)
    rank = jnp.where(present, upto - 1.0 + offset, -1.0)
    places = lax.broadcasted_iota(I32, (512, 512), 1).astype(F32)
    for c in range(4):
        expand[c] = jnp.where(rank[:, c:c + 1] == places, 1.0, 0.0).astype(BF16)
    turned_rank = jnp.transpose(rank)[0:16, :]
    high = jnp.floor(turned_rank * (1.0 / 16.0))
    low = turned_rank - high * 16.0
    own_rank = dot(high.astype(BF16), own_rows) * 16.0 + dot(low.astype(BF16), own_rows)
    is_col = lax.broadcasted_iota(I32, (16, 128), 0) == (jnp.broadcast_to(own_list, (16, 128)) & 3)
    own_rank = jnp.sum(jnp.where(is_col, own_rank, 0.0), axis=0, keepdims=True)
    own_rank = jnp.where(own_list < UNUSED, own_rank, -1.0)
    pool[...] = jnp.where(rows512.astype(F32) == own_rank, 1.0, 0.0).astype(BF16)

    locals_[0].wait()
    for n, j in enumerate((0, 1, 3, 2)):
        locals_[1 + j].wait()
        if j:
            w_copies[4 - j].wait_recv()
        for k in FAR_FIRST:
            x_copies[j, 4 - k].wait_recv()
        part = dot(xs[j], wg[j])
        acc[...] = part if n == 0 else acc[...] + part
    kp_copies = {}
    for k in FAR_FIRST:
        kp_out[k] = acc[k * 128:(k + 1) * 128, :].astype(BF16)
        kp_copies[k] = remote(kp_out.at[k], kp_in.at[4 - k], kp_send.at[k], kp_recv.at[4 - k], along_a(k))
        kp_copies[k].start()
    for j in range(2):
        xt[j] = jnp.transpose(xs[j])
    for k in (1, 3, 2):
        kp_copies[4 - k].wait_recv()
    key_proj = acc[0:128, :]
    for k in (1, 2, 3):
        key_proj = key_proj + kp_in[k].astype(F32)
    slopes[0:128, :] = ((key_proj - tgt_ref[...].astype(F32)) * (1.0 / 128.0)).astype(BF16)
    sl_copies = {}
    for k in FAR_FIRST:
        sl_copies[k] = remote(
            slopes.at[pl.ds(0, 128)], slopes.at[pl.ds((4 - k) * 128, 128)],
            sl_send.at[k], sl_recv.at[4 - k], along_a(k),
        )
        sl_copies[k].start()
    for j in range(2, 4):
        xt[j] = jnp.transpose(xs[j])
    for k in (1, 3, 2):
        sl_copies[4 - k].wait_recv()

    k_copies, g_copies = {}, {}
    for j in (2, 1, 3, 0):
        part = dot(xt[j], slopes[...])
        if j == 0:
            g_own[...] = part
        g_out[j] = part.astype(BF16)
        blocks = jnp.zeros((128, 128), F32)
        for c in range(4):
            blocks = blocks + dot(sel[j, :, c * 512:(c + 1) * 512], g_out[j, :, c * 128:(c + 1) * 128])
        if j == 0:
            for c in range(4):
                blocks = blocks + dot(sel[0, :, c * 512:(c + 1) * 512], fb_ref[:, c * 128:(c + 1) * 128])
            k_own[...] = blocks
        else:
            k_out[j] = blocks.astype(BF16)
            k_copies[j] = remote(k_out.at[j], k_in.at[4 - j], k_send.at[j], k_recv.at[4 - j], along_b(j))
            k_copies[j].start()
    for j in FAR_FIRST:
        g_copies[j] = remote(g_out.at[j], g_in.at[4 - j], g_send.at[j], g_recv.at[4 - j], along_b(j))
        g_copies[j].start()

    for j in (1, 3, 2):
        k_copies[4 - j].wait_recv()
    values = k_own[...]
    for j in (1, 2, 3):
        values = values + k_in[j].astype(F32)
    top = values.astype(BF16)
    rest = (values - top.astype(F32)).astype(BF16)
    both = dot(pool[...], jnp.concatenate([top, rest], axis=1))
    pool_val[...] = both[:, :128] + both[:, 128:]
    mine = pl.multiple_of(core * 256, 256)
    other = pl.multiple_of((1 - core) * 256, 256)
    p_copy = remote(pool_val.at[pl.ds(other, 256)], pool_in, p_send, p_recv, twin)
    p_copy.start()
    p_copy.wait_recv()
    pool_in[...] = pool_in[...] + pool_val[pl.ds(mine, 256), :]
    part16[...] = pool_in[...].astype(BF16)

    @pl.loop(0, 15)
    def _(i):
        k = lax.rem(i + 8, 15) + 1
        to = pl.multiple_of(lax.rem(z + k, 16) * 16, 16)
        remote(part16.at[pl.ds(to, 16)], rs_in.at[16 - k], rs_send.at[k], rs_recv.at[16 - k], along_z(k)).start()

    @pl.loop(1, 16)
    def _(k):
        to = pl.multiple_of(lax.rem(z + k, 16) * 16, 16)
        remote(part16.at[pl.ds(to, 16)], rs_in.at[k], rs_send.at[k], rs_recv.at[k], along_z(k)).wait()

    total = pool_in[pl.ds(pl.multiple_of(z * 16, 16), 16), :]
    for k in range(1, 16):
        total = total + rs_in[k].astype(F32)
    here = pl.multiple_of(core * 256 + z * 16, 16)
    res[pl.ds(here, 16), :] = total * (1.0 / 32.0)

    @pl.loop(0, 15)
    def _(i):
        k = lax.rem(i + 8, 15) + 1
        remote(res.at[pl.ds(here, 16)], res.at[pl.ds(here, 16)], ag_send.at[k], ag_recv.at[16 - k], along_z(k)).start()

    for j in (1, 3, 2):
        g_copies[4 - j].wait_recv()
    whole = g_own[...] + fb_ref[...].astype(F32)
    for j in (1, 2, 3):
        whole = whole + g_in[j].astype(F32)
    newfb_ref[...] = jnp.where(kept[...].astype(F32) > 0.5, 0.0, whole).astype(BF16)

    @pl.loop(1, 16)
    def _(k):
        there = pl.multiple_of(core * 256 + lax.rem(z + k, 16) * 16, 16)
        remote(res.at[pl.ds(here, 16)], res.at[pl.ds(there, 16)], ag_send.at[k], ag_recv.at[k], along_z(k)).wait()

    q_copy = remote(res.at[pl.ds(mine, 256)], res.at[pl.ds(mine, 256)], q_send, q_recv, twin)
    q_copy.start()
    q_copy.wait()
    full = res[...]
    top = full.astype(BF16)
    rest = (full - top.astype(F32)).astype(BF16)
    pair = jnp.concatenate([top, rest], axis=1)
    for c in range(4):
        both = dot(expand[c], pair)
        outer_ref[:, c * 128:(c + 1) * 128] = both[:, :128] + both[:, 128:]

    for copies in (m_copies[:0], w_copies.values(), x_copies.values(), kp_copies.values(), sl_copies.values(),
                   k_copies.values(), g_copies.values()):
        for copy in copies:
            copy.wait_send()
    p_copy.wait_send()


def on_device(inputs, target, weights, feedback, counts, blocks):
    vmem = pl.BlockSpec(memory_space=pltpu.VMEM)
    hbm = pl.BlockSpec(memory_space=pl.ANY)
    sem = pltpu.SemaphoreType.DMA
    outer, newfb = pl.pallas_call(
        kernel,
        out_shape=(jax.ShapeDtypeStruct((512, 512), F32), jax.ShapeDtypeStruct((512, 512), BF16)),
        in_specs=[hbm, vmem, hbm, vmem, pl.BlockSpec(memory_space=pltpu.SMEM), vmem],
        out_specs=(vmem, vmem),
        scratch_shapes=[
            pltpu.VMEM((4, 512, 512), BF16),
            pltpu.VMEM((4, 512, 512), BF16),
            pltpu.VMEM((4, 512, 512), BF16),
            pltpu.VMEM((512, 512), F32),
            pltpu.VMEM((4, 128, 512), BF16),
            pltpu.VMEM((4, 128, 512), BF16),
            pltpu.VMEM((512, 512), BF16),
            pltpu.VMEM((512, 512), F32),
            pltpu.VMEM((4, 512, 512), BF16),
            pltpu.VMEM((4, 512, 512), BF16),
            pltpu.VMEM((4, 128, 128), BF16),
            pltpu.VMEM((4, 128, 128), BF16),
            pltpu.VMEM((128, 128), F32),
            pltpu.VMEM((2, 8, 128), I32),
            pltpu.VMEM((4, 8, 128), I32),
            pltpu.VMEM((16, 8, 128), I32),
            pltpu.VMEM((4, 128, 2048), BF16),
            pltpu.VMEM((4, 512, 512), BF16),
            pltpu.VMEM((512, 128), BF16),
            pltpu.VMEM((512, 512), BF16),
            pltpu.VMEM((512, 128), F32),
            pltpu.VMEM((256, 128), F32),
            pltpu.VMEM((256, 128), BF16),
            pltpu.VMEM((16, 16, 128), BF16),
            pltpu.VMEM((512, 128), F32),
            sem((4, 4)), sem((4, 4)), sem((4,)), sem((4,)), sem((5,)), sem((4,)), sem((4,)), sem((4,)), sem((4,)),
            sem((4,)), sem((4,)), sem((4,)), sem((4,)), sem((4,)), sem((4,)), sem((16,)), sem((16,)),
            sem, sem, sem((16,)), sem((16,)), sem((16,)), sem((16,)), sem, sem,
        ],
        compiler_params=pltpu.CompilerParams(
            collective_id=0, has_side_effects=True, vmem_limit_bytes=56 * 2**20
        ),
        name="outer_sync",
    )(inputs[0], target[0], weights[0], feedback[0], counts, blocks[0])
    return outer, newfb[None]


def solution(mesh):
    placed = (
        P("rep", "shard", None),
        P("rep", "shard", None),
        P("rep", "shard", None),
        P("rep", "shard", None),
        P("rep", "shard"),
        P("rep", "shard", None),
    )
    return jax.shard_map(
        on_device,
        mesh=mesh,
        in_specs=placed,
        out_specs=(P("shard", None), P("rep", "shard", None)),
        check_vma=False,
    )
```

```python
import jax
import jax.numpy as jnp
from jax import lax
from jax.experimental import pallas as pl
from jax.experimental.pallas import tpu as pltpu
from jax.sharding import PartitionSpec as P

MESH = pl.DeviceIdType.MESH
F32, BF16, I32 = jnp.float32, jnp.bfloat16, jnp.int32
UNUSED = 1 << 16
FAR_FIRST = (2, 1, 3)


def dot(a, b):
    return jnp.dot(a, b, preferred_element_type=F32)


def dot_nt(a, b):
    return lax.dot_general(a, b, (((1,), (1,)), ((), ())), preferred_element_type=F32)


def kernel(
    x_ref, tgt_ref, w_ref, fb_ref, cnt_ref, slot_ref,
    res_ref, rank_ref, newfb_ref,
    xs, xt, wg, acc, kp_out, kp_in, slopes, g_out, g_in, k_acc, k_out, k_in,
    meta, meta_b, meta_z, row_sel, col_of, x_sel, k_fb, pool, kept, pool_val, pool_in, part16, rs_in, res,
    tgt, fb, rank_out, newfb,
    x_send, x_recv, w_send, w_recv, loc_sem, kp_send, kp_recv, sl_send, sl_recv,
    g_send, g_recv, k_send, k_recv, m_send, m_recv, mz_send, mz_recv,
    p_send, p_recv, rs_send, rs_recv, ag_send, ag_recv, q_send, q_recv, out_sem, z_sem,
):
    rep, shard = lax.axis_index("rep"), lax.axis_index("shard")
    core, z = lax.rem(rep, 2), rep // 2
    y, x = shard // 4, lax.rem(shard, 4)
    a = x * (1 - core) + y * core
    b = y * (1 - core) + x * core

    def shard_of(aa, bb):
        return (bb * (1 - core) + aa * core) * 4 + (aa * (1 - core) + bb * core)

    def along_a(k):
        return (rep, shard_of(lax.rem(a + k, 4), b))

    def along_b(k):
        return (rep, shard_of(a, lax.rem(b + k, 4)))

    def along_z(k):
        return (lax.rem(rep + 2 * k, 32), shard)

    twin = (rep + 1 - 2 * core, shard)

    def remote(src, dst, send, recv, device):
        return pltpu.make_async_remote_copy(
            src_ref=src, dst_ref=dst, send_sem=send, recv_sem=recv, device_id=device, device_id_type=MESH
        )

    def far_first(i):
        return 8 + ((i + 1) // 2) * (1 - 2 * lax.rem(i + 1, 2))

    barrier = pltpu.get_barrier_semaphore()
    for k in (1, 2, 3):
        pl.semaphore_signal(barrier, inc=1, device_id=along_a(k), device_id_type=MESH)
        pl.semaphore_signal(barrier, inc=1, device_id=along_b(k), device_id_type=MESH)
    for device in (twin, along_z(1), along_z(15)):
        pl.semaphore_signal(barrier, inc=1, device_id=device, device_id_type=MESH)

    locals_ = []
    for j in range(4):
        own = pl.multiple_of(shard_of(a, lax.rem(b + j, 4)) * 512, 512)
        locals_.append(pltpu.make_async_copy(x_ref.at[:, pl.ds(own, 512)], xs.at[j, pl.ds(0, 128)], loc_sem.at[j]))
    locals_.append(pltpu.make_async_copy(w_ref, wg.at[0], loc_sem.at[4]))
    locals_.append(pltpu.make_async_copy(tgt_ref, tgt, loc_sem.at[5]))
    locals_.append(pltpu.make_async_copy(fb_ref, fb, loc_sem.at[6]))
    for copy in locals_:
        copy.start()
    in_use = lax.broadcasted_iota(I32, (8, 128), 1) < jnp.broadcast_to(cnt_ref[...], (8, 128))
    meta[0] = jnp.where(in_use, jnp.broadcast_to(slot_ref[...], (8, 128)), UNUSED)
    pl.semaphore_wait(barrier, 9)

    m_copies = [remote(meta.at[0], meta_b.at[4 - k], m_send.at[k], m_recv.at[4 - k], along_b(k)) for k in (1, 2, 3)]
    m_copies.append(remote(meta.at[0], meta.at[1], m_send.at[0], m_recv.at[0], twin))
    for copy in m_copies:
        copy.start()
    halves = (pl.ds(0, 256), pl.ds(256, 256))
    x_copies, w_copies = {}, {}
    for k, h in ((1, 0), (3, 1), (1, 1), (3, 0)):
        w_copies[k, h] = remote(
            w_ref.at[halves[h]], wg.at[4 - k, halves[h]], w_send.at[k, h], w_recv.at[4 - k, h], along_b(k)
        )
        w_copies[k, h].start()
    for j in (0, 1, 3, 2):
        for k in FAR_FIRST:
            cols = pl.multiple_of(shard_of(lax.rem(a + k, 4), lax.rem(b + j, 4)) * 512, 512)
            x_copies[j, k] = remote(
                x_ref.at[:, pl.ds(cols, 512)], xs.at[j, pl.ds((4 - k) * 128, 128)],
                x_send.at[j, k], x_recv.at[j, 4 - k], along_a(k),
            )
            x_copies[j, k].start()

    for n, step in enumerate((1, 2, 4)):
        for k in (step, 16 - step):
            pl.semaphore_signal(z_sem.at[n], inc=1, device_id=along_z(k), device_id_type=MESH)
        if step < 4:
            pl.semaphore_wait(z_sem.at[n], 2)
    for k, h in ((1, 0), (3, 1)):
        w_copies[k, h].wait_recv()
        w_copies[2, h] = remote(
            wg.at[4 - k, halves[h]], wg.at[2, halves[h]], w_send.at[2, h], w_recv.at[2, h], along_b(k)
        )
        w_copies[2, h].start()
    pl.semaphore_wait(z_sem.at[2], 2)
    m_copies[3].wait()
    row0 = lax.broadcasted_iota(I32, (8, 128), 0) == 0
    meta_z[0] = jnp.where(row0, meta[0], meta[1])

    @pl.loop(1, 16)
    def _(k):
        remote(meta_z.at[0], meta_z.at[16 - k], mz_send.at[k], mz_recv.at[16 - k], along_z(k)).start()

    rows512 = lax.broadcasted_iota(I32, (512, 128), 0)
    lanes512 = lax.broadcasted_iota(I32, (128, 512), 1)
    own_list = meta[0, 0:1, :]
    own_rows = jnp.where(rows512 == (own_list >> 2), 1.0, 0.0).astype(BF16)
    for c in range(4):
        is_c = jnp.where((jnp.broadcast_to(own_list, (128, 128)) & 3) == c, 1.0, 0.0).astype(BF16)
        kept[:, c * 128:(c + 1) * 128] = dot_nt(own_rows, is_c).astype(BF16)
    for k in (1, 2, 3):
        m_copies[k - 1].wait()
    for j in range(4):
        lst = meta[0, 0:1, :] if j == 0 else meta_b[j, 0:1, :]
        turned = jnp.transpose(jnp.broadcast_to(lst, (128, 128)))
        col_of[j] = turned & 3
        row_sel[j] = jnp.where((turned >> 2)[:, 0:1] == lanes512, 1.0, 0.0).astype(BF16)

    def pick(j, part, columns):
        blocks = jnp.zeros((128, 128), F32)
        for n, c in enumerate(columns):
            blocks = blocks + jnp.where(col_of[j] == c, part[:, n * 128:(n + 1) * 128], 0.0)
        return blocks

    for copy in locals_[4:]:
        copy.wait()
    k_fb[...] = pick(0, dot(row_sel[0], fb[...]), range(4))

    def prepare(j):
        xt[j] = jnp.transpose(xs[j])
        x_sel[j * 128:(j + 1) * 128, :] = dot_nt(row_sel[j], xs[j]).astype(BF16)

    for j in (0, 1, 3):
        locals_[j].wait()
        if j == 1:
            w_copies[3, 0].wait_recv()
        elif j == 3:
            w_copies[1, 1].wait_recv()
        for k in FAR_FIRST:
            x_copies[j, 4 - k].wait_recv()
        if j == 0:
            acc[...] = dot(xs[j], wg[j])
        else:
            acc[...] += dot(xs[j], wg[j])
        prepare(j)

    locals_[2].wait()
    w_copies[2, 0].wait_recv()
    w_copies[2, 1].wait_recv()
    for k in FAR_FIRST:
        x_copies[2, 4 - k].wait_recv()
    kp_copies, sl_copies = {}, {}
    for q in range(2):
        cols = slice(q * 256, (q + 1) * 256)
        part = acc[:, cols] + dot(xs[2], wg[2, :, cols])
        acc[0:128, cols] = part[0:128, :]
        for k in FAR_FIRST:
            kp_out[k, q] = part[k * 128:(k + 1) * 128, :].astype(BF16)
            kp_copies[k, q] = remote(
                kp_out.at[k, q], kp_in.at[4 - k, q], kp_send.at[k, q], kp_recv.at[4 - k, q], along_a(k)
            )
            kp_copies[k, q].start()
    prepare(2)

    @pl.loop(1, 16)
    def _(k):
        remote(meta_z.at[0], meta_z.at[16 - k], mz_send.at[k], mz_recv.at[16 - k], along_z(k)).wait_send()
        remote(meta_z.at[0], meta_z.at[k], mz_send.at[k], mz_recv.at[k], along_z(k)).wait_recv()

    def count(i, total):
        lst = jnp.concatenate([meta_z[2 * i + n, r:r + 1, :] for n in (0, 1) for r in (0, 1)], axis=1)
        in_rows = jnp.where(lax.broadcasted_iota(I32, (512, 512), 0) == (lst >> 2), 1.0, 0.0).astype(BF16)
        columns = jnp.broadcast_to(lst, (128, 512)) & 3
        in_cols = jnp.where(lax.broadcasted_iota(I32, (128, 512), 0) == columns, 1.0, 0.0).astype(BF16)
        return total + dot_nt(in_rows, in_cols)

    present = lax.fori_loop(0, 8, count, jnp.zeros((512, 128), F32)) > 0.5
    lower = jnp.where(
        lax.broadcasted_iota(I32, (512, 512), 0) >= lax.broadcasted_iota(I32, (512, 512), 1), 1.0, 0.0
    ).astype(BF16)
    upto = dot(lower, jnp.where(present, 1.0, 0.0).astype(BF16))
    totals = upto[511:512, :]
    lane = lax.broadcasted_iota(I32, (1, 128), 1)
    offset = jnp.zeros((1, 128), F32)
    for c in range(3):
        offset = offset + jnp.where(lane > c, totals[:, c:c + 1], 0.0)
    rank = jnp.where(present, upto - 1.0 + offset, -1.0)
    rank_out[...] = rank
    rank_copy = pltpu.make_async_copy(rank_out, rank_ref, out_sem.at[0])
    rank_copy.start()
    turned_rank = jnp.transpose(rank)[0:16, :]
    high = jnp.floor(turned_rank * (1.0 / 16.0))
    low = turned_rank - high * 16.0
    own_rank = dot(high.astype(BF16), own_rows) * 16.0 + dot(low.astype(BF16), own_rows)
    is_col = lax.broadcasted_iota(I32, (16, 128), 0) == (jnp.broadcast_to(own_list, (16, 128)) & 3)
    own_rank = jnp.sum(jnp.where(is_col, own_rank, 0.0), axis=0, keepdims=True)
    own_rank = jnp.where(own_list < UNUSED, own_rank, -1.0)
    pool[...] = jnp.where(rows512.astype(F32) == own_rank, 1.0, 0.0).astype(BF16)

    for q in range(2):
        cols = slice(q * 256, (q + 1) * 256)
        for k in (1, 3, 2):
            kp_copies[4 - k, q].wait_recv()
        key_proj = acc[0:128, cols]
        for k in (1, 2, 3):
            key_proj = key_proj + kp_in[k, q].astype(F32)
        slopes[q, 0:128, :] = ((key_proj - tgt[:, cols].astype(F32)) * (1.0 / 128.0)).astype(BF16)
        for k in FAR_FIRST:
            sl_copies[k, q] = remote(
                slopes.at[q, pl.ds(0, 128)], slopes.at[q, pl.ds((4 - k) * 128, 128)],
                sl_send.at[k, q], sl_recv.at[4 - k, q], along_a(k),
            )
            sl_copies[k, q].start()

    k_copies, g_copies = {}, {}
    for q in range(2):
        for k in (1, 3, 2):
            sl_copies[4 - k, q].wait_recv()
        part = dot(x_sel[...], slopes[q])
        for j in (2, 1, 3, 0):
            blocks = pick(j, part[j * 128:(j + 1) * 128, :], (2 * q, 2 * q + 1))
            if q == 0:
                k_acc[j] = blocks
            elif j == 0:
                k_acc[0] = k_acc[0] + blocks + k_fb[...]
            else:
                k_out[j] = (k_acc[j] + blocks).astype(BF16)
                k_copies[j] = remote(k_out.at[j], k_in.at[4 - j], k_send.at[j], k_recv.at[4 - j], along_b(j))
                k_copies[j].start()
    for q in range(2):
        for j in FAR_FIRST:
            g_out[j, q] = dot(xt[j], slopes[q]).astype(BF16)
            g_copies[j, q] = remote(
                g_out.at[j, q], g_in.at[4 - j, q], g_send.at[j, q], g_recv.at[4 - j, q], along_b(j)
            )
            g_copies[j, q].start()

    for j in (1, 3, 2):
        k_copies[4 - j].wait_recv()
    values = k_acc[0]
    for j in (1, 2, 3):
        values = values + k_in[j].astype(F32)
    top = values.astype(BF16)
    rest = (values - top.astype(F32)).astype(BF16)
    both = dot(pool[...], jnp.concatenate([top, rest], axis=1))
    pool_val[...] = both[:, :128] + both[:, 128:]
    mine = pl.multiple_of(core * 256, 256)
    other = pl.multiple_of((1 - core) * 256, 256)
    p_copy = remote(pool_val.at[pl.ds(other, 256)], pool_in, p_send, p_recv, twin)
    p_copy.start()
    p_copy.wait_recv()
    pool_in[...] = pool_in[...] + pool_val[pl.ds(mine, 256), :]
    part16[...] = pool_in[...].astype(BF16)

    @pl.loop(0, 15)
    def _(i):
        k = far_first(i)
        to = pl.multiple_of(lax.rem(z + k, 16) * 16, 16)
        remote(part16.at[pl.ds(to, 16)], rs_in.at[16 - k], rs_send.at[k], rs_recv.at[16 - k], along_z(k)).start()

    @pl.loop(1, 16)
    def _(k):
        to = pl.multiple_of(lax.rem(z + k, 16) * 16, 16)
        remote(part16.at[pl.ds(to, 16)], rs_in.at[k], rs_send.at[k], rs_recv.at[k], along_z(k)).wait()

    here = pl.multiple_of(z * 16, 16)
    total = pool_in[pl.ds(here, 16), :]
    for k in range(1, 16):
        total = total + rs_in[k].astype(F32)
    res[pl.ds(here, 16), :] = (total * (1.0 / 32.0)).astype(BF16)

    @pl.loop(0, 15)
    def _(i):
        k = far_first(i)
        remote(res.at[pl.ds(here, 16)], res.at[pl.ds(here, 16)], ag_send.at[k], ag_recv.at[16 - k], along_z(k)).start()

    for q in range(2):
        cols = slice(q * 256, (q + 1) * 256)
        whole = dot(xt[0], slopes[q]) + fb[:, cols].astype(F32)
        for j in (1, 3, 2):
            g_copies[4 - j, q].wait_recv()
        for j in (1, 2, 3):
            whole = whole + g_in[j, q].astype(F32)
        newfb[:, cols] = jnp.where(kept[:, cols].astype(F32) > 0.5, 0.0, whole).astype(BF16)
    newfb_copy = pltpu.make_async_copy(newfb, newfb_ref, out_sem.at[1])
    newfb_copy.start()
    for copies in (w_copies, x_copies, kp_copies, sl_copies, k_copies, g_copies):
        for copy in copies.values():
            copy.wait_send()
    p_copy.wait_send()
    rank_copy.wait()

    @pl.loop(1, 16)
    def _(k):
        there = pl.multiple_of(lax.rem(z + k, 16) * 16, 16)
        remote(res.at[pl.ds(here, 16)], res.at[pl.ds(there, 16)], ag_send.at[k], ag_recv.at[k], along_z(k)).wait()

    q_copy = remote(res, res_ref.at[pl.ds(mine, 256)], q_send, q_recv, twin)
    q_copy.start()
    res_copy = pltpu.make_async_copy(res, res_ref.at[pl.ds(mine, 256)], out_sem.at[2])
    res_copy.start()
    newfb_copy.wait()
    res_copy.wait()
    q_copy.wait()


def expand(res_ref, rank_ref, newfb_ref, outer_ref, newfb_out_ref, res, rank, newfb, outer, sems):
    res_copy = pltpu.make_async_copy(res_ref, res, sems.at[0])
    rank_copy = pltpu.make_async_copy(rank_ref, rank, sems.at[1])
    newfb_copy = pltpu.make_async_copy(newfb_ref, newfb, sems.at[2])
    newfb_out_copy = pltpu.make_async_copy(newfb, newfb_out_ref, sems.at[7])
    rank_copy.start()
    res_copy.start()
    newfb_copy.start()
    rank_copy.wait()
    res_copy.wait()
    places = lax.broadcasted_iota(I32, (128, 512), 1).astype(F32)
    copies = []
    for r in range(4):
        rows = slice(r * 128, (r + 1) * 128)
        if r == 1:
            newfb_copy.wait()
            newfb_out_copy.start()
        for c in range(4):
            one_hot = jnp.where(rank[rows, c:c + 1] == places, 1.0, 0.0).astype(BF16)
            outer[rows, c * 128:(c + 1) * 128] = dot(one_hot, res[...])
        copies.append(pltpu.make_async_copy(
            outer.at[pl.ds(r * 128, 128)], outer_ref.at[pl.ds(r * 128, 128)], sems.at[3 + r]
        ))
        copies[r].start()
    for copy in copies:
        copy.wait()
    newfb_out_copy.wait()


def on_device(inputs, target, weights, feedback, counts, blocks):
    vmem = pl.BlockSpec(memory_space=pltpu.VMEM)
    hbm = pl.BlockSpec(memory_space=pl.ANY)
    sem = pltpu.SemaphoreType.DMA
    res, rank, newfb = pl.pallas_call(
        kernel,
        out_shape=(
            jax.ShapeDtypeStruct((512, 128), BF16),
            jax.ShapeDtypeStruct((512, 128), F32),
            jax.ShapeDtypeStruct((512, 512), BF16),
        ),
        in_specs=[hbm, hbm, hbm, hbm, vmem, vmem],
        out_specs=(hbm, hbm, hbm),
        scratch_shapes=[
            pltpu.VMEM((4, 512, 512), BF16),
            pltpu.VMEM((4, 512, 512), BF16),
            pltpu.VMEM((4, 512, 512), BF16),
            pltpu.VMEM((512, 512), F32),
            pltpu.VMEM((4, 2, 128, 256), BF16),
            pltpu.VMEM((4, 2, 128, 256), BF16),
            pltpu.VMEM((2, 512, 256), BF16),
            pltpu.VMEM((4, 2, 512, 256), BF16),
            pltpu.VMEM((4, 2, 512, 256), BF16),
            pltpu.VMEM((4, 128, 128), F32),
            pltpu.VMEM((4, 128, 128), BF16),
            pltpu.VMEM((4, 128, 128), BF16),
            pltpu.VMEM((2, 8, 128), I32),
            pltpu.VMEM((4, 8, 128), I32),
            pltpu.VMEM((16, 8, 128), I32),
            pltpu.VMEM((4, 128, 512), BF16),
            pltpu.VMEM((4, 128, 128), I32),
            pltpu.VMEM((512, 512), BF16),
            pltpu.VMEM((128, 128), F32),
            pltpu.VMEM((512, 128), BF16),
            pltpu.VMEM((512, 512), BF16),
            pltpu.VMEM((512, 128), F32),
            pltpu.VMEM((256, 128), F32),
            pltpu.VMEM((256, 128), BF16),
            pltpu.VMEM((16, 16, 128), BF16),
            pltpu.VMEM((256, 128), BF16),
            pltpu.VMEM((128, 512), BF16),
            pltpu.VMEM((512, 512), BF16),
            pltpu.VMEM((512, 128), F32),
            pltpu.VMEM((512, 512), BF16),
            sem((4, 4)), sem((4, 4)),
            sem((4, 2)), sem((4, 2)),
            sem((7,)),
            sem((4, 2)), sem((4, 2)),
            sem((4, 2)), sem((4, 2)),
            sem((4, 2)), sem((4, 2)),
            sem((4,)), sem((4,)),
            sem((4,)), sem((4,)),
            sem((16,)), sem((16,)),
            sem, sem,
            sem((16,)), sem((16,)),
            sem((16,)), sem((16,)),
            sem, sem,
            sem((3,)),
            pltpu.SemaphoreType.REGULAR((3,)),
        ],
        compiler_params=pltpu.CompilerParams(
            collective_id=0, has_side_effects=True, vmem_limit_bytes=56 * 2**20
        ),
        name="outer_sync",
    )(inputs[0], target[0], weights[0], feedback[0], counts, blocks[0])
    outer, newfb = pl.pallas_call(
        expand,
        out_shape=(jax.ShapeDtypeStruct((512, 512), F32), jax.ShapeDtypeStruct((512, 512), BF16)),
        in_specs=[hbm, hbm, hbm],
        out_specs=(hbm, hbm),
        scratch_shapes=[
            pltpu.VMEM((512, 128), BF16), pltpu.VMEM((512, 128), F32), pltpu.VMEM((512, 512), BF16),
            pltpu.VMEM((512, 512), F32), sem((8,)),
        ],
        compiler_params=pltpu.CompilerParams(vmem_limit_bytes=56 * 2**20),
        name="expand_pool",
    )(res, rank, newfb)
    return outer, newfb[None]


def solution(mesh):
    placed = (
        P("rep", "shard", None),
        P("rep", "shard", None),
        P("rep", "shard", None),
        P("rep", "shard", None),
        P("rep", "shard"),
        P("rep", "shard", None),
    )
    return jax.shard_map(
        on_device,
        mesh=mesh,
        in_specs=placed,
        out_specs=(P("shard", None), P("rep", "shard", None)),
        check_vma=False,
    )
```

```python
import jax
import jax.numpy as jnp
from jax import lax
from jax.experimental import pallas as pl
from jax.experimental.pallas import tpu as pltpu
from jax.sharding import PartitionSpec as P

MESH = pl.DeviceIdType.MESH
F32, BF16, I32 = jnp.float32, jnp.bfloat16, jnp.int32
UNUSED = 1 << 16
FAR_FIRST = (2, 1, 3)


def dot(a, b):
    return jnp.dot(a, b, preferred_element_type=F32)


def dot_nt(a, b):
    return lax.dot_general(a, b, (((1,), (1,)), ((), ())), preferred_element_type=F32)


def kernel(
    x_ref, tgt_ref, w_ref, fb_ref, cnt_ref, slot_ref,
    res_ref, rank_ref, newfb_ref,
    xs, xt, wg, acc, kp_out, kp_in, slopes, g_own, g_out, g_in, k_acc, k_out, k_in,
    meta, meta_b, meta_z, row_sel, col_of, x_sel, k_fb, pool, kept, pool_val, pool_in, part16, rs_in, res,
    tgt, fb, slot, cnt, rank_out, newfb,
    x_send, x_recv, w_send, w_recv, loc_sem, kp_send, kp_recv, sl_send, sl_recv,
    g_send, g_recv, k_send, k_recv, m_send, m_recv, mt_send, mt_recv, mz_send, mz_recv,
    p_send, p_recv, rs_send, rs_recv, ag_send, ag_recv, q_send, q_recv, out_sem, z_sem,
):
    rep, shard = lax.axis_index("rep"), lax.axis_index("shard")
    core, z = lax.rem(rep, 2), rep // 2
    y, x = shard // 4, lax.rem(shard, 4)
    a = x * (1 - core) + y * core
    b = y * (1 - core) + x * core

    def shard_of(aa, bb):
        return (bb * (1 - core) + aa * core) * 4 + (aa * (1 - core) + bb * core)

    def along_a(k):
        return (rep, shard_of(lax.rem(a + k, 4), b))

    def along_b(k):
        return (rep, shard_of(a, lax.rem(b + k, 4)))

    def along_z(k):
        return (lax.rem(rep + 2 * k, 32), shard)

    twin = (rep + 1 - 2 * core, shard)

    def remote(src, dst, send, recv, device):
        return pltpu.make_async_remote_copy(
            src_ref=src, dst_ref=dst, send_sem=send, recv_sem=recv, device_id=device, device_id_type=MESH
        )

    def sent(view, sem):
        remote(view, view, sem, sem, twin).wait_send()

    def arrived(view, sem):
        remote(view, view, sem, sem, twin).wait_recv()

    def far_first(i):
        return 8 + ((i + 1) // 2) * (1 - 2 * lax.rem(i + 1, 2))

    barrier = pltpu.get_barrier_semaphore()
    for k in (1, 2, 3):
        pl.semaphore_signal(barrier, inc=1, device_id=along_a(k), device_id_type=MESH)
        pl.semaphore_signal(barrier, inc=1, device_id=along_b(k), device_id_type=MESH)
    for device in (twin, along_z(1), along_z(15)):
        pl.semaphore_signal(barrier, inc=1, device_id=device, device_id_type=MESH)

    lists = [
        pltpu.make_async_copy(slot_ref, slot, loc_sem.at[4]), pltpu.make_async_copy(cnt_ref, cnt, loc_sem.at[5])
    ]
    for copy in lists:
        copy.start()
    for j in range(4):
        own = pl.multiple_of(shard_of(a, lax.rem(b + j, 4)) * 512, 512)
        pltpu.make_async_copy(x_ref.at[:, pl.ds(own, 512)], xs.at[j, pl.ds(0, 128)], loc_sem.at[0]).start()
    own_tokens = xs.at[:, pl.ds(0, 128)]
    locals_ = [
        pltpu.make_async_copy(w_ref, wg.at[0], loc_sem.at[1]),
        pltpu.make_async_copy(tgt_ref, tgt, loc_sem.at[2]),
        pltpu.make_async_copy(fb_ref, fb, loc_sem.at[3]),
    ]
    for copy in locals_:
        copy.start()
    for copy in lists:
        copy.wait()
    in_use = lax.broadcasted_iota(I32, (8, 128), 1) < jnp.broadcast_to(cnt[...], (8, 128))
    meta[0] = jnp.where(in_use, jnp.broadcast_to(slot[...], (8, 128)), UNUSED)
    pl.semaphore_wait(barrier, 9)

    for k in (1, 2, 3):
        remote(meta.at[0], meta_b.at[4 - k], m_send, m_recv, along_b(k)).start()
    m_copy = remote(meta.at[0], meta.at[1], mt_send, mt_recv, twin)
    m_copy.start()
    halves = (pl.ds(0, 256), pl.ds(256, 256))
    for k, h in ((1, 0), (3, 1), (1, 1), (3, 0)):
        remote(
            w_ref.at[halves[h]], wg.at[4 - k, halves[h]], w_send, w_recv.at[4 - k, h], along_b(k)
        ).start()
    for j in (0, 1, 3, 2):
        for k in FAR_FIRST:
            cols = pl.multiple_of(shard_of(lax.rem(a + k, 4), lax.rem(b + j, 4)) * 512, 512)
            remote(
                x_ref.at[:, pl.ds(cols, 512)], xs.at[j, pl.ds((4 - k) * 128, 128)], x_send, x_recv.at[j], along_a(k)
            ).start()

    for n, step in enumerate((1, 2, 4)):
        for k in (step, 16 - step):
            pl.semaphore_signal(z_sem.at[n], inc=1, device_id=along_z(k), device_id_type=MESH)
        if step < 4:
            pl.semaphore_wait(z_sem.at[n], 2)
    for k, h in ((1, 0), (3, 1)):
        arrived(wg.at[4 - k, halves[h]], w_recv.at[4 - k, h])
        remote(wg.at[4 - k, halves[h]], wg.at[2, halves[h]], w_send, w_recv.at[2, 0], along_b(k)).start()
    pl.semaphore_wait(z_sem.at[2], 2)
    m_copy.wait()
    row0 = lax.broadcasted_iota(I32, (8, 128), 0) == 0
    meta_z[0] = jnp.where(row0, meta[0], meta[1])

    @pl.loop(1, 16)
    def _(k):
        remote(meta_z.at[0], meta_z.at[16 - k], mz_send, mz_recv, along_z(k)).start()

    rows512 = lax.broadcasted_iota(I32, (512, 128), 0)
    lanes512 = lax.broadcasted_iota(I32, (128, 512), 1)
    own_list = meta[0, 0:1, :]
    own_rows = jnp.where(rows512 == (own_list >> 2), 1.0, 0.0).astype(BF16)
    for c in range(4):
        is_c = jnp.where((jnp.broadcast_to(own_list, (128, 128)) & 3) == c, 1.0, 0.0).astype(BF16)
        kept[:, c * 128:(c + 1) * 128] = dot_nt(own_rows, is_c).astype(BF16)
    arrived(meta_b.at[pl.ds(1, 3)], m_recv)
    for j in range(4):
        lst = meta[0, 0:1, :] if j == 0 else meta_b[j, 0:1, :]
        turned = jnp.transpose(jnp.broadcast_to(lst, (128, 128)))
        col_of[j] = turned & 3
        row_sel[j] = jnp.where((turned >> 2)[:, 0:1] == lanes512, 1.0, 0.0).astype(BF16)

    def pick(j, part, columns):
        blocks = jnp.zeros((128, 128), F32)
        for n, c in enumerate(columns):
            blocks = blocks + jnp.where(col_of[j] == c, part[:, n * 128:(n + 1) * 128], 0.0)
        return blocks

    for copy in locals_:
        copy.wait()
    pltpu.make_async_copy(own_tokens, own_tokens, loc_sem.at[0]).wait()
    k_fb[...] = pick(0, dot(row_sel[0], fb[...]), range(4))

    def prepare(j):
        xt[j] = jnp.transpose(xs[j])
        x_sel[j * 128:(j + 1) * 128, :] = dot_nt(row_sel[j], xs[j]).astype(BF16)

    for j in (0, 1, 3):
        if j == 1:
            arrived(wg.at[1, halves[0]], w_recv.at[1, 0])
        elif j == 3:
            arrived(wg.at[3, halves[1]], w_recv.at[3, 1])
        arrived(xs.at[j, pl.ds(128, 384)], x_recv.at[j])
        if j == 0:
            acc[...] = dot(xs[j], wg[j])
        else:
            acc[...] += dot(xs[j], wg[j])
        prepare(j)

    arrived(meta_z.at[pl.ds(1, 15)], mz_recv)

    def count(i, total):
        lst = jnp.concatenate([meta_z[2 * i + n, r:r + 1, :] for n in (0, 1) for r in (0, 1)], axis=1)
        in_rows = jnp.where(lax.broadcasted_iota(I32, (512, 512), 0) == (lst >> 2), 1.0, 0.0).astype(BF16)
        columns = jnp.broadcast_to(lst, (128, 512)) & 3
        in_cols = jnp.where(lax.broadcasted_iota(I32, (128, 512), 0) == columns, 1.0, 0.0).astype(BF16)
        return total + dot_nt(in_rows, in_cols)

    present = lax.fori_loop(0, 8, count, jnp.zeros((512, 128), F32)) > 0.5
    arrived(wg.at[2], w_recv.at[2, 0])
    arrived(xs.at[2, pl.ds(128, 384)], x_recv.at[2])
    for q in range(2):
        cols = slice(q * 256, (q + 1) * 256)
        part = acc[:, cols] + dot(xs[2], wg[2, :, cols])
        acc[0:128, cols] = part[0:128, :]
        for k in FAR_FIRST:
            kp_out[q, k] = part[k * 128:(k + 1) * 128, :].astype(BF16)
            remote(kp_out.at[q, k], kp_in.at[q, 4 - k], kp_send, kp_recv.at[q], along_a(k)).start()
    prepare(2)

    lower = jnp.where(
        lax.broadcasted_iota(I32, (512, 512), 0) >= lax.broadcasted_iota(I32, (512, 512), 1), 1.0, 0.0
    ).astype(BF16)
    upto = dot(lower, jnp.where(present, 1.0, 0.0).astype(BF16))
    totals = upto[511:512, :]
    lane = lax.broadcasted_iota(I32, (1, 128), 1)
    offset = jnp.zeros((1, 128), F32)
    for c in range(3):
        offset = offset + jnp.where(lane > c, totals[:, c:c + 1], 0.0)
    rank = jnp.where(present, upto - 1.0 + offset, -1.0)
    rank_out[...] = rank
    rank_copy = pltpu.make_async_copy(rank_out, rank_ref, out_sem.at[0])
    rank_copy.start()
    turned_rank = jnp.transpose(rank)[0:16, :]
    high = jnp.floor(turned_rank * (1.0 / 16.0))
    low = turned_rank - high * 16.0
    own_rank = dot(high.astype(BF16), own_rows) * 16.0 + dot(low.astype(BF16), own_rows)
    is_col = lax.broadcasted_iota(I32, (16, 128), 0) == (jnp.broadcast_to(own_list, (16, 128)) & 3)
    own_rank = jnp.sum(jnp.where(is_col, own_rank, 0.0), axis=0, keepdims=True)
    own_rank = jnp.where(own_list < UNUSED, own_rank, -1.0)
    pool[...] = jnp.where(rows512.astype(F32) == own_rank, 1.0, 0.0).astype(BF16)

    for q in range(2):
        cols = slice(q * 256, (q + 1) * 256)
        arrived(kp_in.at[q, pl.ds(1, 3)], kp_recv.at[q])
        key_proj = acc[0:128, cols]
        for k in (1, 2, 3):
            key_proj = key_proj + kp_in[q, k].astype(F32)
        slopes[q, 0:128, :] = ((key_proj - tgt[:, cols].astype(F32)) * (1.0 / 128.0)).astype(BF16)
        for k in FAR_FIRST:
            remote(
                slopes.at[q, pl.ds(0, 128)], slopes.at[q, pl.ds((4 - k) * 128, 128)], sl_send, sl_recv.at[q], along_a(k)
            ).start()

    for q in range(2):
        arrived(slopes.at[q, pl.ds(128, 384)], sl_recv.at[q])
        part = dot(x_sel[...], slopes[q])
        for j in (2, 1, 3, 0):
            blocks = pick(j, part[j * 128:(j + 1) * 128, :], (2 * q, 2 * q + 1))
            if q == 0:
                k_acc[j] = blocks
            elif j == 0:
                k_acc[0] = k_acc[0] + blocks + k_fb[...]
            else:
                k_out[j] = (k_acc[j] + blocks).astype(BF16)
                remote(k_out.at[j], k_in.at[4 - j], k_send, k_recv, along_b(j)).start()
    for q in range(2):
        for j in FAR_FIRST:
            g_out[q, j] = dot(xt[j], slopes[q]).astype(BF16)

    arrived(k_in.at[pl.ds(1, 3)], k_recv)
    values = k_acc[0]
    for j in (1, 2, 3):
        values = values + k_in[j].astype(F32)
    top = values.astype(BF16)
    rest = (values - top.astype(F32)).astype(BF16)
    both = dot(pool[...], jnp.concatenate([top, rest], axis=1))
    pool_val[...] = both[:, :128] + both[:, 128:]
    mine = pl.multiple_of(core * 256, 256)
    other = pl.multiple_of((1 - core) * 256, 256)
    p_copy = remote(pool_val.at[pl.ds(other, 256)], pool_in, p_send, p_recv, twin)
    p_copy.start()
    p_copy.wait_recv()
    pool_in[...] = pool_in[...] + pool_val[pl.ds(mine, 256), :]
    part16[...] = pool_in[...].astype(BF16)

    @pl.loop(0, 15)
    def _(i):
        k = far_first(i)
        to = pl.multiple_of(lax.rem(z + k, 16) * 16, 16)
        remote(part16.at[pl.ds(to, 16)], rs_in.at[16 - k], rs_send, rs_recv, along_z(k)).start()

    for q in range(2):
        for j in FAR_FIRST:
            remote(g_out.at[q, j], g_in.at[q, 4 - j], g_send, g_recv.at[q], along_b(j)).start()

    for q in range(2):
        g_own[q] = dot(xt[0], slopes[q])

    arrived(rs_in.at[pl.ds(1, 15)], rs_recv)
    here = pl.multiple_of(z * 16, 16)
    total = pool_in[pl.ds(here, 16), :]
    for k in range(1, 16):
        total = total + rs_in[k].astype(F32)
    res[pl.ds(here, 16), :] = (total * (1.0 / 32.0)).astype(BF16)

    @pl.loop(0, 15)
    def _(i):
        k = far_first(i)
        remote(res.at[pl.ds(here, 16)], res.at[pl.ds(here, 16)], ag_send, ag_recv, along_z(k)).start()

    arrived(res.at[pl.ds(0, 240)], ag_recv)
    q_copy = remote(res, res_ref.at[pl.ds(mine, 256)], q_send, q_recv, twin)
    q_copy.start()
    res_copy = pltpu.make_async_copy(res, res_ref.at[pl.ds(mine, 256)], out_sem.at[2])
    res_copy.start()

    for q in range(2):
        cols = slice(q * 256, (q + 1) * 256)
        whole = g_own[q] + fb[:, cols].astype(F32)
        arrived(g_in.at[q, pl.ds(1, 3)], g_recv.at[q])
        for j in (1, 2, 3):
            whole = whole + g_in[q, j].astype(F32)
        newfb[:, cols] = jnp.where(kept[:, cols].astype(F32) > 0.5, 0.0, whole).astype(BF16)
    newfb_copy = pltpu.make_async_copy(newfb, newfb_ref, out_sem.at[1])
    newfb_copy.start()
    sent(xs.at[pl.ds(0, 3)], x_send)
    sent(wg.at[pl.ds(0, 3)], w_send)
    sent(meta_b.at[pl.ds(1, 3)], m_send)
    sent(meta_z.at[pl.ds(1, 15)], mz_send)
    sent(kp_in.at[:, pl.ds(1, 3)], kp_send)
    sent(slopes.at[:, pl.ds(128, 384)], sl_send)
    sent(k_in.at[pl.ds(1, 3)], k_send)
    sent(g_in.at[:, pl.ds(1, 3)], g_send)
    sent(rs_in.at[pl.ds(1, 15)], rs_send)
    sent(res.at[pl.ds(0, 240)], ag_send)
    p_copy.wait_send()
    rank_copy.wait()
    res_copy.wait()
    q_copy.wait()
    newfb_copy.wait()


def expand(res_ref, rank_ref, newfb_ref, outer_ref, newfb_out_ref, res, rank, newfb, outer, sems):
    res_copy = pltpu.make_async_copy(res_ref, res, sems.at[0])
    rank_copy = pltpu.make_async_copy(rank_ref, rank, sems.at[1])
    newfb_copy = pltpu.make_async_copy(newfb_ref, newfb, sems.at[2])
    newfb_out_copy = pltpu.make_async_copy(newfb, newfb_out_ref, sems.at[7])
    rank_copy.start()
    res_copy.start()
    newfb_copy.start()
    rank_copy.wait()
    res_copy.wait()
    places = lax.broadcasted_iota(I32, (128, 512), 1).astype(F32)
    copies = []
    for r in range(4):
        rows = slice(r * 128, (r + 1) * 128)
        if r == 1:
            newfb_copy.wait()
            newfb_out_copy.start()
        for c in range(4):
            one_hot = jnp.where(rank[rows, c:c + 1] == places, 1.0, 0.0).astype(BF16)
            outer[rows, c * 128:(c + 1) * 128] = dot(one_hot, res[...])
        copies.append(pltpu.make_async_copy(
            outer.at[pl.ds(r * 128, 128)], outer_ref.at[pl.ds(r * 128, 128)], sems.at[3 + r]
        ))
        copies[r].start()
    for copy in copies:
        copy.wait()
    newfb_out_copy.wait()


def on_device(inputs, target, weights, feedback, counts, blocks):
    hbm = pl.BlockSpec(memory_space=pl.ANY)
    sem = pltpu.SemaphoreType.DMA
    res, rank, newfb = pl.pallas_call(
        kernel,
        out_shape=(
            jax.ShapeDtypeStruct((512, 128), BF16),
            jax.ShapeDtypeStruct((512, 128), F32),
            jax.ShapeDtypeStruct((512, 512), BF16),
        ),
        in_specs=[hbm] * 6,
        out_specs=(hbm, hbm, hbm),
        scratch_shapes=[
            pltpu.VMEM((4, 512, 512), BF16),
            pltpu.VMEM((4, 512, 512), BF16),
            pltpu.VMEM((4, 512, 512), BF16),
            pltpu.VMEM((512, 512), F32),
            pltpu.VMEM((2, 4, 128, 256), BF16),
            pltpu.VMEM((2, 4, 128, 256), BF16),
            pltpu.VMEM((2, 512, 256), BF16),
            pltpu.VMEM((2, 512, 256), F32),
            pltpu.VMEM((2, 4, 512, 256), BF16),
            pltpu.VMEM((2, 4, 512, 256), BF16),
            pltpu.VMEM((4, 128, 128), F32),
            pltpu.VMEM((4, 128, 128), BF16),
            pltpu.VMEM((4, 128, 128), BF16),
            pltpu.VMEM((2, 8, 128), I32),
            pltpu.VMEM((4, 8, 128), I32),
            pltpu.VMEM((16, 8, 128), I32),
            pltpu.VMEM((4, 128, 512), BF16),
            pltpu.VMEM((4, 128, 128), I32),
            pltpu.VMEM((512, 512), BF16),
            pltpu.VMEM((128, 128), F32),
            pltpu.VMEM((512, 128), BF16),
            pltpu.VMEM((512, 512), BF16),
            pltpu.VMEM((512, 128), F32),
            pltpu.VMEM((256, 128), F32),
            pltpu.VMEM((256, 128), BF16),
            pltpu.VMEM((16, 16, 128), BF16),
            pltpu.VMEM((256, 128), BF16),
            pltpu.VMEM((128, 512), BF16),
            pltpu.VMEM((512, 512), BF16),
            pltpu.VMEM((1, 128), I32),
            pltpu.VMEM((1, 1), I32),
            pltpu.VMEM((512, 128), F32),
            pltpu.VMEM((512, 512), BF16),
            sem, sem((4,)),
            sem, sem((4, 2)),
            sem((6,)),
            sem, sem((2,)),
            sem, sem((2,)),
            sem, sem((2,)),
            sem, sem,
            sem, sem, sem, sem,
            sem, sem,
            sem, sem,
            sem, sem,
            sem, sem,
            sem, sem,
            sem((3,)),
            pltpu.SemaphoreType.REGULAR((3,)),
        ],
        compiler_params=pltpu.CompilerParams(
            collective_id=0, has_side_effects=True, vmem_limit_bytes=56 * 2**20
        ),
        name="outer_sync",
    )(inputs[0], target[0], weights[0], feedback[0], counts, blocks[0])
    outer, newfb = pl.pallas_call(
        expand,
        out_shape=(jax.ShapeDtypeStruct((512, 512), F32), jax.ShapeDtypeStruct((512, 512), BF16)),
        in_specs=[hbm, hbm, hbm],
        out_specs=(hbm, hbm),
        scratch_shapes=[
            pltpu.VMEM((512, 128), BF16), pltpu.VMEM((512, 128), F32), pltpu.VMEM((512, 512), BF16),
            pltpu.VMEM((512, 512), F32), sem((8,)),
        ],
        compiler_params=pltpu.CompilerParams(vmem_limit_bytes=56 * 2**20),
        name="expand_pool",
    )(res, rank, newfb)
    return outer, newfb[None]


def solution(mesh):
    placed = (
        P("rep", "shard", None),
        P("rep", "shard", None),
        P("rep", "shard", None),
        P("rep", "shard", None),
        P("rep", "shard"),
        P("rep", "shard", None),
    )
    return jax.shard_map(
        on_device,
        mesh=mesh,
        in_specs=placed,
        out_specs=(P("shard", None), P("rep", "shard", None)),
        check_vma=False,
    )
```

```python
import jax
import jax.numpy as jnp
from jax import lax
from jax.experimental import pallas as pl
from jax.experimental.pallas import tpu as pltpu
from jax.sharding import PartitionSpec as P

MESH = pl.DeviceIdType.MESH
F32, BF16, I32 = jnp.float32, jnp.bfloat16, jnp.int32
UNUSED = 1 << 16
FAR_FIRST = (2, 1, 3)


def dot(a, b):
    return jnp.dot(a, b, preferred_element_type=F32)


def dot_nt(a, b):
    return lax.dot_general(a, b, (((1,), (1,)), ((), ())), preferred_element_type=F32)


def kernel(
    x_ref, tgt_ref, w_ref, fb_ref, cnt_ref, slot_ref,
    res_ref, rank_ref, newfb_ref,
    xs, xt, wg, acc, kp_out, kp_in, slopes, g_own, g_out, g_in, k_acc, k_out, k_in,
    meta, meta_b, meta_z, row_sel, col_of, x_sel, k_fb, pool, kept, pool_val, pool_in, part16, rs_in, res,
    tgt, fb, slot, cnt, rank_out, newfb,
    x_send, x_recv, w_send, w_recv, loc_sem, kp_send, kp_recv, sl_send, sl_recv,
    g_send, g_recv, k_send, k_recv, m_send, m_recv, mt_send, mt_recv, mz_send, mz_recv,
    p_send, p_recv, rs_send, rs_recv, ag_send, ag_recv, q_send, q_recv, out_sem, z_sem,
):
    rep, shard = lax.axis_index("rep"), lax.axis_index("shard")
    core, z = lax.rem(rep, 2), rep // 2
    y, x = shard // 4, lax.rem(shard, 4)
    a = x * (1 - core) + y * core
    b = y * (1 - core) + x * core

    def shard_of(aa, bb):
        return (bb * (1 - core) + aa * core) * 4 + (aa * (1 - core) + bb * core)

    def along_a(k):
        return (rep, shard_of(lax.rem(a + k, 4), b))

    def along_b(k):
        return (rep, shard_of(a, lax.rem(b + k, 4)))

    def along_z(k):
        return (lax.rem(rep + 2 * k, 32), shard)

    twin = (rep + 1 - 2 * core, shard)

    def remote(src, dst, send, recv, device):
        return pltpu.make_async_remote_copy(
            src_ref=src, dst_ref=dst, send_sem=send, recv_sem=recv, device_id=device, device_id_type=MESH
        )

    def sent(view, sem):
        remote(view, view, sem, sem, twin).wait_send()

    def arrived(view, sem):
        remote(view, view, sem, sem, twin).wait_recv()

    def far_first(i):
        return 8 + ((i + 1) // 2) * (1 - 2 * lax.rem(i + 1, 2))

    barrier = pltpu.get_barrier_semaphore()
    for k in (1, 2, 3):
        pl.semaphore_signal(barrier, inc=1, device_id=along_a(k), device_id_type=MESH)
        pl.semaphore_signal(barrier, inc=1, device_id=along_b(k), device_id_type=MESH)
    for device in (twin, along_z(1), along_z(15)):
        pl.semaphore_signal(barrier, inc=1, device_id=device, device_id_type=MESH)

    lists = [
        pltpu.make_async_copy(slot_ref, slot, loc_sem.at[4]), pltpu.make_async_copy(cnt_ref, cnt, loc_sem.at[5])
    ]
    for copy in lists:
        copy.start()
    for j in range(4):
        own = pl.multiple_of(shard_of(a, lax.rem(b + j, 4)) * 512, 512)
        pltpu.make_async_copy(x_ref.at[:, pl.ds(own, 512)], xs.at[j, pl.ds(0, 128)], loc_sem.at[0]).start()
    own_tokens = xs.at[:, pl.ds(0, 128)]
    locals_ = [
        pltpu.make_async_copy(w_ref, wg.at[0], loc_sem.at[1]),
        pltpu.make_async_copy(tgt_ref, tgt, loc_sem.at[2]),
        pltpu.make_async_copy(fb_ref, fb, loc_sem.at[3]),
    ]
    for copy in locals_:
        copy.start()
    for copy in lists:
        copy.wait()
    in_use = lax.broadcasted_iota(I32, (8, 128), 1) < jnp.broadcast_to(cnt[...], (8, 128))
    meta[0] = jnp.where(in_use, jnp.broadcast_to(slot[...], (8, 128)), UNUSED)
    pl.semaphore_wait(barrier, 9)

    for k in (1, 2, 3):
        remote(meta.at[0], meta_b.at[4 - k], m_send, m_recv, along_b(k)).start()
    m_copy = remote(meta.at[0], meta.at[1], mt_send, mt_recv, twin)
    m_copy.start()
    halves = (pl.ds(0, 256), pl.ds(256, 256))
    for k, h in ((1, 0), (3, 1), (1, 1), (3, 0)):
        remote(
            w_ref.at[halves[h]], wg.at[4 - k, halves[h]], w_send, w_recv.at[4 - k, h], along_b(k)
        ).start()
    for j in (0, 1, 3, 2):
        for k in FAR_FIRST:
            cols = pl.multiple_of(shard_of(lax.rem(a + k, 4), lax.rem(b + j, 4)) * 512, 512)
            remote(
                x_ref.at[:, pl.ds(cols, 512)], xs.at[j, pl.ds((4 - k) * 128, 128)], x_send, x_recv.at[j], along_a(k)
            ).start()

    for n, step in enumerate((1, 2, 4)):
        for k in (step, 16 - step):
            pl.semaphore_signal(z_sem.at[n], inc=1, device_id=along_z(k), device_id_type=MESH)
        if step < 4:
            pl.semaphore_wait(z_sem.at[n], 2)
    for k, h in ((1, 0), (3, 1)):
        arrived(wg.at[4 - k, halves[h]], w_recv.at[4 - k, h])
        remote(wg.at[4 - k, halves[h]], wg.at[2, halves[h]], w_send, w_recv.at[2, 0], along_b(k)).start()
    pl.semaphore_wait(z_sem.at[2], 2)
    m_copy.wait()
    row0 = lax.broadcasted_iota(I32, (8, 128), 0) == 0
    meta_z[0] = jnp.where(row0, meta[0], meta[1])

    @pl.loop(1, 16)
    def _(k):
        remote(meta_z.at[0], meta_z.at[16 - k], mz_send, mz_recv, along_z(k)).start()

    rows512 = lax.broadcasted_iota(I32, (512, 128), 0)
    lanes512 = lax.broadcasted_iota(I32, (128, 512), 1)
    own_list = meta[0, 0:1, :]
    own_rows = jnp.where(rows512 == (own_list >> 2), 1.0, 0.0).astype(BF16)
    for c in range(4):
        is_c = jnp.where((jnp.broadcast_to(own_list, (128, 128)) & 3) == c, 1.0, 0.0).astype(BF16)
        kept[:, c * 128:(c + 1) * 128] = dot_nt(own_rows, is_c).astype(BF16)
    arrived(meta_b.at[pl.ds(1, 3)], m_recv)
    for j in range(4):
        lst = meta[0, 0:1, :] if j == 0 else meta_b[j, 0:1, :]
        turned = jnp.transpose(jnp.broadcast_to(lst, (128, 128)))
        col_of[j] = turned & 3
        row_sel[j] = jnp.where((turned >> 2)[:, 0:1] == lanes512, 1.0, 0.0).astype(BF16)

    def pick(j, part, columns):
        blocks = jnp.zeros((128, 128), F32)
        for n, c in enumerate(columns):
            blocks = blocks + jnp.where(col_of[j] == c, part[:, n * 128:(n + 1) * 128], 0.0)
        return blocks

    for copy in locals_:
        copy.wait()
    pltpu.make_async_copy(own_tokens, own_tokens, loc_sem.at[0]).wait()
    k_fb[...] = pick(0, dot(row_sel[0], fb[...]), range(4))

    def prepare(j):
        xt[j] = jnp.transpose(xs[j])
        x_sel[j * 128:(j + 1) * 128, :] = dot_nt(row_sel[j], xs[j]).astype(BF16)

    for j in (0, 1, 3):
        if j == 1:
            arrived(wg.at[1, halves[0]], w_recv.at[1, 0])
        elif j == 3:
            arrived(wg.at[3, halves[1]], w_recv.at[3, 1])
        arrived(xs.at[j, pl.ds(128, 384)], x_recv.at[j])
        if j == 0:
            acc[...] = dot(xs[j], wg[j])
        else:
            acc[...] += dot(xs[j], wg[j])
        prepare(j)

    arrived(meta_z.at[pl.ds(1, 15)], mz_recv)

    def count(i, total):
        lst = jnp.concatenate([meta_z[2 * i + n, r:r + 1, :] for n in (0, 1) for r in (0, 1)], axis=1)
        in_rows = jnp.where(lax.broadcasted_iota(I32, (512, 512), 0) == (lst >> 2), 1.0, 0.0).astype(BF16)
        columns = jnp.broadcast_to(lst, (128, 512)) & 3
        in_cols = jnp.where(lax.broadcasted_iota(I32, (128, 512), 0) == columns, 1.0, 0.0).astype(BF16)
        return total + dot_nt(in_rows, in_cols)

    present = lax.fori_loop(0, 8, count, jnp.zeros((512, 128), F32)) > 0.5
    arrived(wg.at[2], w_recv.at[2, 0])
    arrived(xs.at[2, pl.ds(128, 384)], x_recv.at[2])
    for q in range(2):
        cols = slice(q * 256, (q + 1) * 256)
        part = acc[:, cols] + dot(xs[2], wg[2, :, cols])
        acc[0:128, cols] = part[0:128, :]
        for k in FAR_FIRST:
            kp_out[q, k] = part[k * 128:(k + 1) * 128, :].astype(BF16)
            remote(kp_out.at[q, k], kp_in.at[q, 4 - k], kp_send, kp_recv.at[q], along_a(k)).start()
    prepare(2)

    lower = jnp.where(
        lax.broadcasted_iota(I32, (512, 512), 0) >= lax.broadcasted_iota(I32, (512, 512), 1), 1.0, 0.0
    ).astype(BF16)
    upto = dot(lower, jnp.where(present, 1.0, 0.0).astype(BF16))
    totals = upto[511:512, :]
    lane = lax.broadcasted_iota(I32, (1, 128), 1)
    offset = jnp.zeros((1, 128), F32)
    for c in range(3):
        offset = offset + jnp.where(lane > c, totals[:, c:c + 1], 0.0)
    rank = jnp.where(present, upto - 1.0 + offset, -1.0)
    rank_out[...] = rank
    rank_copy = pltpu.make_async_copy(rank_out, rank_ref, out_sem.at[0])
    rank_copy.start()
    turned_rank = jnp.transpose(rank)[0:16, :]
    high = jnp.floor(turned_rank * (1.0 / 16.0))
    low = turned_rank - high * 16.0
    own_rank = dot(high.astype(BF16), own_rows) * 16.0 + dot(low.astype(BF16), own_rows)
    is_col = lax.broadcasted_iota(I32, (16, 128), 0) == (jnp.broadcast_to(own_list, (16, 128)) & 3)
    own_rank = jnp.sum(jnp.where(is_col, own_rank, 0.0), axis=0, keepdims=True)
    own_rank = jnp.where(own_list < UNUSED, own_rank, -1.0)
    pool[...] = jnp.where(rows512.astype(F32) == own_rank, 1.0, 0.0).astype(BF16)

    for q in range(2):
        cols = slice(q * 256, (q + 1) * 256)
        arrived(kp_in.at[q, pl.ds(1, 3)], kp_recv.at[q])
        key_proj = acc[0:128, cols]
        for k in (1, 2, 3):
            key_proj = key_proj + kp_in[q, k].astype(F32)
        slopes[q, 0:128, :] = ((key_proj - tgt[:, cols].astype(F32)) * (1.0 / 128.0)).astype(BF16)
        for k in FAR_FIRST:
            remote(
                slopes.at[q, pl.ds(0, 128)], slopes.at[q, pl.ds((4 - k) * 128, 128)], sl_send, sl_recv.at[q], along_a(k)
            ).start()

    for q in range(2):
        arrived(slopes.at[q, pl.ds(128, 384)], sl_recv.at[q])
        part = dot(x_sel[...], slopes[q])
        for j in (2, 1, 3, 0):
            blocks = pick(j, part[j * 128:(j + 1) * 128, :], (2 * q, 2 * q + 1))
            if q == 0:
                k_acc[j] = blocks
            elif j == 0:
                k_acc[0] = k_acc[0] + blocks + k_fb[...]
            else:
                k_out[j] = (k_acc[j] + blocks).astype(BF16)
                remote(k_out.at[j], k_in.at[4 - j], k_send, k_recv, along_b(j)).start()
    for q in range(2):
        for j in FAR_FIRST:
            g_out[q, j] = dot(xt[j], slopes[q]).astype(BF16)

    arrived(k_in.at[pl.ds(1, 3)], k_recv)
    values = k_acc[0]
    for j in (1, 2, 3):
        values = values + k_in[j].astype(F32)
    top = values.astype(BF16)
    rest = (values - top.astype(F32)).astype(BF16)
    both = dot(pool[...], jnp.concatenate([top, rest], axis=1))
    pool_val[...] = both[:, :128] + both[:, 128:]
    mine = pl.multiple_of(core * 256, 256)
    other = pl.multiple_of((1 - core) * 256, 256)
    p_copy = remote(pool_val.at[pl.ds(other, 256)], pool_in, p_send, p_recv, twin)
    p_copy.start()
    p_copy.wait_recv()
    pool_in[...] = pool_in[...] + pool_val[pl.ds(mine, 256), :]
    part16[...] = pool_in[...].astype(BF16)

    @pl.loop(0, 15)
    def _(i):
        k = far_first(i)
        to = pl.multiple_of(lax.rem(z + k, 16) * 16, 16)
        remote(part16.at[pl.ds(to, 16)], rs_in.at[16 - k], rs_send, rs_recv, along_z(k)).start()

    for q in range(2):
        for j in FAR_FIRST:
            remote(g_out.at[q, j], g_in.at[q, 4 - j], g_send, g_recv.at[q], along_b(j)).start()

    for q in range(2):
        g_own[q] = dot(xt[0], slopes[q])

    arrived(rs_in.at[pl.ds(1, 15)], rs_recv)
    here = pl.multiple_of(z * 16, 16)
    total = pool_in[pl.ds(here, 16), :]
    for k in range(1, 16):
        total = total + rs_in[k].astype(F32)
    res[pl.ds(here, 16), :] = (total * (1.0 / 32.0)).astype(BF16)

    @pl.loop(0, 15)
    def _(i):
        k = far_first(i)
        remote(res.at[pl.ds(here, 16)], res.at[pl.ds(here, 16)], ag_send, ag_recv, along_z(k)).start()

    arrived(res.at[pl.ds(0, 240)], ag_recv)
    q_copy = remote(res, res_ref.at[pl.ds(mine, 256)], q_send, q_recv, twin)
    q_copy.start()
    res_copy = pltpu.make_async_copy(res, res_ref.at[pl.ds(mine, 256)], out_sem.at[2])
    res_copy.start()

    for q in range(2):
        cols = slice(q * 256, (q + 1) * 256)
        whole = g_own[q] + fb[:, cols].astype(F32)
        arrived(g_in.at[q, pl.ds(1, 3)], g_recv.at[q])
        for j in (1, 2, 3):
            whole = whole + g_in[q, j].astype(F32)
        newfb[:, cols] = jnp.where(kept[:, cols].astype(F32) > 0.5, 0.0, whole).astype(BF16)
    newfb_copy = pltpu.make_async_copy(newfb, newfb_ref, out_sem.at[1])
    newfb_copy.start()
    sent(xs.at[pl.ds(0, 3)], x_send)
    sent(wg.at[pl.ds(0, 3)], w_send)
    sent(meta_b.at[pl.ds(1, 3)], m_send)
    sent(meta_z.at[pl.ds(1, 15)], mz_send)
    sent(kp_in.at[:, pl.ds(1, 3)], kp_send)
    sent(slopes.at[:, pl.ds(128, 384)], sl_send)
    sent(k_in.at[pl.ds(1, 3)], k_send)
    sent(g_in.at[:, pl.ds(1, 3)], g_send)
    sent(rs_in.at[pl.ds(1, 15)], rs_send)
    sent(res.at[pl.ds(0, 240)], ag_send)
    p_copy.wait_send()
    rank_copy.wait()
    res_copy.wait()
    q_copy.wait()
    newfb_copy.wait()


def expand(res, rank, newfb, outer_ref, newfb_out_ref, outer, sems):
    newfb_copy = pltpu.make_async_copy(newfb, newfb_out_ref, sems.at[4])
    newfb_copy.start()
    places = lax.broadcasted_iota(I32, (128, 512), 1).astype(F32)
    copies = []
    for r in range(4):
        rows = slice(r * 128, (r + 1) * 128)
        for c in range(4):
            one_hot = jnp.where(rank[rows, c:c + 1] == places, 1.0, 0.0).astype(BF16)
            outer[rows, c * 128:(c + 1) * 128] = dot(one_hot, res[...])
        copies.append(pltpu.make_async_copy(
            outer.at[pl.ds(r * 128, 128)], outer_ref.at[pl.ds(r * 128, 128)], sems.at[r]
        ))
        copies[r].start()
    for copy in copies:
        copy.wait()
    newfb_copy.wait()


def on_device(inputs, target, weights, feedback, counts, blocks):
    hbm = pl.BlockSpec(memory_space=pl.ANY)
    sem = pltpu.SemaphoreType.DMA
    operands = (inputs[0], target[0], weights[0], feedback[0], counts, blocks[0])
    res, rank, newfb = pl.pallas_call(
        kernel,
        out_shape=(
            jax.ShapeDtypeStruct((512, 128), BF16),
            jax.ShapeDtypeStruct((512, 128), F32),
            jax.ShapeDtypeStruct((512, 512), BF16),
        ),
        in_specs=[hbm] * 6,
        out_specs=(hbm, hbm, hbm),
        scratch_shapes=[
            pltpu.VMEM((4, 512, 512), BF16),
            pltpu.VMEM((4, 512, 512), BF16),
            pltpu.VMEM((4, 512, 512), BF16),
            pltpu.VMEM((512, 512), F32),
            pltpu.VMEM((2, 4, 128, 256), BF16),
            pltpu.VMEM((2, 4, 128, 256), BF16),
            pltpu.VMEM((2, 512, 256), BF16),
            pltpu.VMEM((2, 512, 256), F32),
            pltpu.VMEM((2, 4, 512, 256), BF16),
            pltpu.VMEM((2, 4, 512, 256), BF16),
            pltpu.VMEM((4, 128, 128), F32),
            pltpu.VMEM((4, 128, 128), BF16),
            pltpu.VMEM((4, 128, 128), BF16),
            pltpu.VMEM((2, 8, 128), I32),
            pltpu.VMEM((4, 8, 128), I32),
            pltpu.VMEM((16, 8, 128), I32),
            pltpu.VMEM((4, 128, 512), BF16),
            pltpu.VMEM((4, 128, 128), I32),
            pltpu.VMEM((512, 512), BF16),
            pltpu.VMEM((128, 128), F32),
            pltpu.VMEM((512, 128), BF16),
            pltpu.VMEM((512, 512), BF16),
            pltpu.VMEM((512, 128), F32),
            pltpu.VMEM((256, 128), F32),
            pltpu.VMEM((256, 128), BF16),
            pltpu.VMEM((16, 16, 128), BF16),
            pltpu.VMEM((256, 128), BF16),
            pltpu.VMEM((128, 512), BF16),
            pltpu.VMEM((512, 512), BF16),
            pltpu.VMEM((1, 128), I32),
            pltpu.VMEM((1, 1), I32),
            pltpu.VMEM((512, 128), F32),
            pltpu.VMEM((512, 512), BF16),
            sem, sem((4,)),
            sem, sem((4, 2)),
            sem((6,)),
            sem, sem((2,)),
            sem, sem((2,)),
            sem, sem((2,)),
            sem, sem,
            sem, sem, sem, sem,
            sem, sem,
            sem, sem,
            sem, sem,
            sem, sem,
            sem, sem,
            sem((3,)),
            pltpu.SemaphoreType.REGULAR((3,)),
        ],
        compiler_params=pltpu.CompilerParams(
            collective_id=0, has_side_effects=True, vmem_limit_bytes=40 * 2**20
        ),
        name="outer_sync",
    )(*[v if v.size == 1 else pltpu.with_memory_space_constraint(v, pltpu.HBM) for v in operands])
    outer, newfb = pl.pallas_call(
        expand,
        out_shape=(jax.ShapeDtypeStruct((512, 512), F32), jax.ShapeDtypeStruct((512, 512), BF16)),
        in_specs=[pl.BlockSpec(memory_space=pltpu.VMEM)] * 3,
        out_specs=(hbm, hbm),
        scratch_shapes=[pltpu.VMEM((512, 512), F32), sem((5,))],
        compiler_params=pltpu.CompilerParams(vmem_limit_bytes=8 * 2**20),
        name="expand_pool",
    )(*[pltpu.with_memory_space_constraint(v, pltpu.VMEM) for v in (res, rank, newfb)])
    return outer, newfb[None]


def solution(mesh):
    placed = (
        P("rep", "shard", None),
        P("rep", "shard", None),
        P("rep", "shard", None),
        P("rep", "shard", None),
        P("rep", "shard"),
        P("rep", "shard", None),
    )
    return jax.shard_map(
        on_device,
        mesh=mesh,
        in_specs=placed,
        out_specs=(P("shard", None), P("rep", "shard", None)),
        check_vma=False,
    )
```

```python
import jax
import jax.numpy as jnp
from jax import lax
from jax.experimental import pallas as pl
from jax.experimental.pallas import tpu as pltpu
from jax.sharding import PartitionSpec as P

MESH = pl.DeviceIdType.MESH
F32, BF16, I32 = jnp.float32, jnp.bfloat16, jnp.int32
UNUSED = 1 << 16
FAR_FIRST = (2, 1, 3)


def dot(a, b):
    return jnp.dot(a, b, preferred_element_type=F32)


def dot_nt(a, b):
    return lax.dot_general(a, b, (((1,), (1,)), ((), ())), preferred_element_type=F32)


def kernel(
    x_ref, tgt_ref, w_ref, fb_ref, cnt_ref, slot_ref,
    res_ref, rank_ref, newfb_ref,
    xs, xt, wg, acc, kp_out, kp_in, slopes, g_own, g_out, g_in, k_acc, k_out, k_in,
    meta, meta_b, meta_z, row_sel, col_of, x_sel, k_fb, pool, kept, pool_val, pool_in, part16, rs_in, res,
    tgt, fb, slot, cnt,
    x_send, x_recv, w_send, w_recv, loc_sem, kp_send, kp_recv, sl_send, sl_recv,
    g_send, g_recv, k_send, k_recv, m_send, m_recv, mt_send, mt_recv, mz_send, mz_recv,
    p_send, p_recv, rs_send, rs_recv, ag_send, ag_recv, q_send, q_recv, out_sem, z_sem,
):
    rep, shard = lax.axis_index("rep"), lax.axis_index("shard")
    core, z = lax.rem(rep, 2), rep // 2
    y, x = shard // 4, lax.rem(shard, 4)
    a = x * (1 - core) + y * core
    b = y * (1 - core) + x * core

    def shard_of(aa, bb):
        return (bb * (1 - core) + aa * core) * 4 + (aa * (1 - core) + bb * core)

    def along_a(k):
        return (rep, shard_of(lax.rem(a + k, 4), b))

    def along_b(k):
        return (rep, shard_of(a, lax.rem(b + k, 4)))

    def along_z(k):
        return (lax.rem(rep + 2 * k, 32), shard)

    twin = (rep + 1 - 2 * core, shard)

    def remote(src, dst, send, recv, device):
        return pltpu.make_async_remote_copy(
            src_ref=src, dst_ref=dst, send_sem=send, recv_sem=recv, device_id=device, device_id_type=MESH
        )

    def sent(view, sem):
        remote(view, view, sem, sem, twin).wait_send()

    def arrived(view, sem):
        remote(view, view, sem, sem, twin).wait_recv()

    def far_first(i):
        return 8 + ((i + 1) // 2) * (1 - 2 * lax.rem(i + 1, 2))

    barrier = pltpu.get_barrier_semaphore()
    for k in (1, 2, 3):
        pl.semaphore_signal(barrier, inc=1, device_id=along_a(k), device_id_type=MESH)
        pl.semaphore_signal(barrier, inc=1, device_id=along_b(k), device_id_type=MESH)
    for device in (twin, along_z(1), along_z(15)):
        pl.semaphore_signal(barrier, inc=1, device_id=device, device_id_type=MESH)

    lists = [
        pltpu.make_async_copy(slot_ref, slot, loc_sem.at[4]), pltpu.make_async_copy(cnt_ref, cnt, loc_sem.at[5])
    ]
    for copy in lists:
        copy.start()
    for j in range(4):
        own = pl.multiple_of(shard_of(a, lax.rem(b + j, 4)) * 512, 512)
        pltpu.make_async_copy(x_ref.at[:, pl.ds(own, 512)], xs.at[j, pl.ds(0, 128)], loc_sem.at[0]).start()
    own_tokens = xs.at[:, pl.ds(0, 128)]
    locals_ = [
        pltpu.make_async_copy(w_ref, wg.at[0], loc_sem.at[1]),
        pltpu.make_async_copy(tgt_ref, tgt, loc_sem.at[2]),
        pltpu.make_async_copy(fb_ref, fb, loc_sem.at[3]),
    ]
    for copy in locals_:
        copy.start()
    for copy in lists:
        copy.wait()
    in_use = lax.broadcasted_iota(I32, (8, 128), 1) < jnp.broadcast_to(cnt[...], (8, 128))
    meta[0] = jnp.where(in_use, jnp.broadcast_to(slot[...], (8, 128)), UNUSED)
    pl.semaphore_wait(barrier, 9)

    for k in (1, 2, 3):
        remote(meta.at[0], meta_b.at[4 - k], m_send, m_recv, along_b(k)).start()
    m_copy = remote(meta.at[0], meta.at[1], mt_send, mt_recv, twin)
    m_copy.start()
    halves = (pl.ds(0, 256), pl.ds(256, 256))
    for k, h in ((1, 0), (3, 1), (1, 1), (3, 0)):
        remote(
            w_ref.at[halves[h]], wg.at[4 - k, halves[h]], w_send, w_recv.at[4 - k, h], along_b(k)
        ).start()
    for j in (0, 1, 3, 2):
        for k in FAR_FIRST:
            cols = pl.multiple_of(shard_of(lax.rem(a + k, 4), lax.rem(b + j, 4)) * 512, 512)
            remote(
                x_ref.at[:, pl.ds(cols, 512)], xs.at[j, pl.ds((4 - k) * 128, 128)], x_send, x_recv.at[j], along_a(k)
            ).start()

    for n, step in enumerate((1, 2, 4)):
        for k in (step, 16 - step):
            pl.semaphore_signal(z_sem.at[n], inc=1, device_id=along_z(k), device_id_type=MESH)
        if step < 4:
            pl.semaphore_wait(z_sem.at[n], 2)
    for k, h in ((1, 0), (3, 1)):
        arrived(wg.at[4 - k, halves[h]], w_recv.at[4 - k, h])
        remote(wg.at[4 - k, halves[h]], wg.at[2, halves[h]], w_send, w_recv.at[2, 0], along_b(k)).start()
    pl.semaphore_wait(z_sem.at[2], 2)
    m_copy.wait()
    row0 = lax.broadcasted_iota(I32, (8, 128), 0) == 0
    meta_z[0] = jnp.where(row0, meta[0], meta[1])

    @pl.loop(1, 16)
    def _(k):
        remote(meta_z.at[0], meta_z.at[16 - k], mz_send, mz_recv, along_z(k)).start()

    rows512 = lax.broadcasted_iota(I32, (512, 128), 0)
    lanes512 = lax.broadcasted_iota(I32, (128, 512), 1)
    own_list = meta[0, 0:1, :]
    own_rows = jnp.where(rows512 == (own_list >> 2), 1.0, 0.0).astype(BF16)
    for c in range(4):
        is_c = jnp.where((jnp.broadcast_to(own_list, (128, 128)) & 3) == c, 1.0, 0.0).astype(BF16)
        kept[:, c * 128:(c + 1) * 128] = dot_nt(own_rows, is_c).astype(BF16)
    arrived(meta_b.at[pl.ds(1, 3)], m_recv)
    for j in range(4):
        lst = meta[0, 0:1, :] if j == 0 else meta_b[j, 0:1, :]
        turned = jnp.transpose(jnp.broadcast_to(lst, (128, 128)))
        col_of[j] = turned & 3
        row_sel[j] = jnp.where((turned >> 2)[:, 0:1] == lanes512, 1.0, 0.0).astype(BF16)

    def pick(j, part, columns):
        blocks = jnp.zeros((128, 128), F32)
        for n, c in enumerate(columns):
            blocks = blocks + jnp.where(col_of[j] == c, part[:, n * 128:(n + 1) * 128], 0.0)
        return blocks

    for copy in locals_:
        copy.wait()
    pltpu.make_async_copy(own_tokens, own_tokens, loc_sem.at[0]).wait()
    k_fb[...] = pick(0, dot(row_sel[0], fb[...]), range(4))

    def prepare(j):
        xt[j] = jnp.transpose(xs[j])
        x_sel[j * 128:(j + 1) * 128, :] = dot_nt(row_sel[j], xs[j]).astype(BF16)

    for j in (0, 1, 3):
        if j == 1:
            arrived(wg.at[1, halves[0]], w_recv.at[1, 0])
        elif j == 3:
            arrived(wg.at[3, halves[1]], w_recv.at[3, 1])
        arrived(xs.at[j, pl.ds(128, 384)], x_recv.at[j])
        if j == 0:
            acc[...] = dot(xs[j], wg[j])
        else:
            acc[...] += dot(xs[j], wg[j])
        prepare(j)

    arrived(meta_z.at[pl.ds(1, 15)], mz_recv)

    def count(i, total):
        lst = jnp.concatenate([meta_z[2 * i + n, r:r + 1, :] for n in (0, 1) for r in (0, 1)], axis=1)
        in_rows = jnp.where(lax.broadcasted_iota(I32, (512, 512), 0) == (lst >> 2), 1.0, 0.0).astype(BF16)
        columns = jnp.broadcast_to(lst, (128, 512)) & 3
        in_cols = jnp.where(lax.broadcasted_iota(I32, (128, 512), 0) == columns, 1.0, 0.0).astype(BF16)
        return total + dot_nt(in_rows, in_cols)

    present = lax.fori_loop(0, 8, count, jnp.zeros((512, 128), F32)) > 0.5
    arrived(wg.at[2], w_recv.at[2, 0])
    arrived(xs.at[2, pl.ds(128, 384)], x_recv.at[2])
    @pl.loop(0, 2)
    def _(q):
        cols = pl.ds(pl.multiple_of(q * 256, 256), 256)
        part = acc[:, cols] + dot(xs[2], wg[2, :, cols])
        acc[0:128, cols] = part[0:128, :]
        for h in range(2):
            p = 2 * q + h
            for k in FAR_FIRST:
                kp_out[p, k] = part[k * 128:(k + 1) * 128, h * 128:(h + 1) * 128].astype(BF16)
                remote(kp_out.at[p, k], kp_in.at[p, 4 - k], kp_send, kp_recv.at[p], along_a(k)).start()
    prepare(2)

    lower = jnp.where(
        lax.broadcasted_iota(I32, (512, 512), 0) >= lax.broadcasted_iota(I32, (512, 512), 1), 1.0, 0.0
    ).astype(BF16)
    upto = dot(lower, jnp.where(present, 1.0, 0.0).astype(BF16))
    totals = upto[511:512, :]
    lane = lax.broadcasted_iota(I32, (1, 128), 1)
    offset = jnp.zeros((1, 128), F32)
    for c in range(3):
        offset = offset + jnp.where(lane > c, totals[:, c:c + 1], 0.0)
    rank = jnp.where(present, upto - 1.0 + offset, -1.0)
    rank_ref[...] = rank
    turned_rank = jnp.transpose(rank)[0:16, :]
    high = jnp.floor(turned_rank * (1.0 / 16.0))
    low = turned_rank - high * 16.0
    own_rank = dot(high.astype(BF16), own_rows) * 16.0 + dot(low.astype(BF16), own_rows)
    is_col = lax.broadcasted_iota(I32, (16, 128), 0) == (jnp.broadcast_to(own_list, (16, 128)) & 3)
    own_rank = jnp.sum(jnp.where(is_col, own_rank, 0.0), axis=0, keepdims=True)
    own_rank = jnp.where(own_list < UNUSED, own_rank, -1.0)
    pool[...] = jnp.where(rows512.astype(F32) == own_rank, 1.0, 0.0).astype(BF16)

    for p in range(4):
        cols, lanes = slice(p * 128, (p + 1) * 128), pl.ds(p % 2 * 128, 128)
        arrived(kp_in.at[p, pl.ds(1, 3)], kp_recv.at[p])
        key_proj = acc[0:128, cols]
        for k in (1, 2, 3):
            key_proj = key_proj + kp_in[p, k].astype(F32)
        slopes[p // 2, 0:128, lanes] = ((key_proj - tgt[:, cols].astype(F32)) * (1.0 / 128.0)).astype(BF16)
        for k in FAR_FIRST:
            remote(
                slopes.at[p // 2, pl.ds(0, 128), lanes], slopes.at[p // 2, pl.ds((4 - k) * 128, 128), lanes],
                sl_send, sl_recv.at[p], along_a(k),
            ).start()

    k_acc[...] = jnp.zeros_like(k_acc)
    k_acc[0] = k_fb[...]

    @pl.loop(0, 2)
    def _(q):
        for h in range(2):
            arrived(slopes.at[q, pl.ds(128, 384), pl.ds(h * 128, 128)], sl_recv.at[2 * q + h])
        part = dot(x_sel[...], slopes[q])
        for j in range(4):
            k_acc[j] += pick(j, part[j * 128:(j + 1) * 128, :], (2 * q, 2 * q + 1))

    for j in FAR_FIRST:
        k_out[j] = k_acc[j].astype(BF16)
        remote(k_out.at[j], k_in.at[4 - j], k_send, k_recv, along_b(j)).start()

    @pl.loop(0, 6)
    def _(i):
        q, j = i // 3, lax.rem(i, 3) + 1
        g_out[q, j] = dot(xt[j], slopes[q]).astype(BF16)

    arrived(k_in.at[pl.ds(1, 3)], k_recv)
    values = k_acc[0]
    for j in (1, 2, 3):
        values = values + k_in[j].astype(F32)
    top = values.astype(BF16)
    rest = (values - top.astype(F32)).astype(BF16)
    both = dot(pool[...], jnp.concatenate([top, rest], axis=1))
    pool_val[...] = both[:, :128] + both[:, 128:]
    mine = pl.multiple_of(core * 256, 256)
    other = pl.multiple_of((1 - core) * 256, 256)
    p_copy = remote(pool_val.at[pl.ds(other, 256)], pool_in, p_send, p_recv, twin)
    p_copy.start()
    p_copy.wait_recv()
    pool_in[...] = pool_in[...] + pool_val[pl.ds(mine, 256), :]
    part16[...] = pool_in[...].astype(BF16)

    @pl.loop(0, 15)
    def _(i):
        k = far_first(i)
        to = pl.multiple_of(lax.rem(z + k, 16) * 16, 16)
        remote(part16.at[pl.ds(to, 16)], rs_in.at[16 - k], rs_send, rs_recv, along_z(k)).start()

    for q in range(2):
        for j in FAR_FIRST:
            remote(g_out.at[q, j], g_in.at[q, 4 - j], g_send, g_recv.at[q], along_b(j)).start()

    @pl.loop(0, 2)
    def _(q):
        g_own[q] = dot(xt[0], slopes[q])

    arrived(rs_in.at[pl.ds(1, 15)], rs_recv)
    here = pl.multiple_of(z * 16, 16)
    total = pool_in[pl.ds(here, 16), :]
    for k in range(1, 16):
        total = total + rs_in[k].astype(F32)
    res[pl.ds(here, 16), :] = (total * (1.0 / 32.0)).astype(BF16)

    @pl.loop(0, 15)
    def _(i):
        k = far_first(i)
        remote(res.at[pl.ds(here, 16)], res.at[pl.ds(here, 16)], ag_send, ag_recv, along_z(k)).start()

    arrived(res.at[pl.ds(0, 240)], ag_recv)
    q_copy = remote(res, res_ref.at[pl.ds(mine, 256)], q_send, q_recv, twin)
    q_copy.start()
    res_copy = pltpu.make_async_copy(res, res_ref.at[pl.ds(mine, 256)], out_sem.at[0])
    res_copy.start()

    @pl.loop(0, 2)
    def _(q):
        cols = pl.ds(pl.multiple_of(q * 256, 256), 256)
        whole = g_own[q] + fb[:, cols].astype(F32)
        arrived(g_in.at[q, pl.ds(1, 3)], g_recv.at[q])
        for j in (1, 2, 3):
            whole = whole + g_in[q, j].astype(F32)
        newfb_ref[:, cols] = jnp.where(kept[:, cols].astype(F32) > 0.5, 0.0, whole).astype(BF16)
    sent(xs.at[pl.ds(0, 3)], x_send)
    sent(wg.at[pl.ds(0, 3)], w_send)
    sent(meta_b.at[pl.ds(1, 3)], m_send)
    sent(meta_z.at[pl.ds(1, 15)], mz_send)
    sent(kp_in.at[:, pl.ds(1, 3)], kp_send)
    sent(slopes.at[:, pl.ds(128, 384)], sl_send)
    sent(k_in.at[pl.ds(1, 3)], k_send)
    sent(g_in.at[:, pl.ds(1, 3)], g_send)
    sent(rs_in.at[pl.ds(1, 15)], rs_send)
    sent(res.at[pl.ds(0, 240)], ag_send)
    p_copy.wait_send()
    res_copy.wait()
    q_copy.wait()


def expand(res, rank, newfb, outer_ref, newfb_out_ref, outer, sems):
    newfb_copy = pltpu.make_async_copy(newfb, newfb_out_ref, sems.at[4])
    newfb_copy.start()
    places = lax.broadcasted_iota(I32, (128, 512), 1).astype(F32)
    copies = []
    for r in range(4):
        rows = slice(r * 128, (r + 1) * 128)
        for c in range(4):
            one_hot = jnp.where(rank[rows, c:c + 1] == places, 1.0, 0.0).astype(BF16)
            outer[rows, c * 128:(c + 1) * 128] = dot(one_hot, res[...])
        copies.append(pltpu.make_async_copy(
            outer.at[pl.ds(r * 128, 128)], outer_ref.at[pl.ds(r * 128, 128)], sems.at[r]
        ))
        copies[r].start()
    for copy in copies:
        copy.wait()
    newfb_copy.wait()


def on_device(inputs, target, weights, feedback, counts, blocks):
    hbm = pl.BlockSpec(memory_space=pl.ANY)
    sem = pltpu.SemaphoreType.DMA
    operands = (inputs[0], target[0], weights[0], feedback[0], counts, blocks[0])
    res, rank, newfb = pl.pallas_call(
        kernel,
        out_shape=(
            pltpu.VMEM((512, 128), BF16),
            pltpu.VMEM((512, 128), F32),
            pltpu.VMEM((512, 512), BF16),
        ),
        in_specs=[hbm] * 6,
        out_specs=(pl.BlockSpec(memory_space=pltpu.VMEM),) * 3,
        scratch_shapes=[
            pltpu.VMEM((4, 512, 512), BF16),
            pltpu.VMEM((4, 512, 512), BF16),
            pltpu.VMEM((4, 512, 512), BF16),
            pltpu.VMEM((512, 512), F32),
            pltpu.VMEM((4, 4, 128, 128), BF16),
            pltpu.VMEM((4, 4, 128, 128), BF16),
            pltpu.VMEM((2, 512, 256), BF16),
            pltpu.VMEM((2, 512, 256), F32),
            pltpu.VMEM((2, 4, 512, 256), BF16),
            pltpu.VMEM((2, 4, 512, 256), BF16),
            pltpu.VMEM((4, 128, 128), F32),
            pltpu.VMEM((4, 128, 128), BF16),
            pltpu.VMEM((4, 128, 128), BF16),
            pltpu.VMEM((2, 8, 128), I32),
            pltpu.VMEM((4, 8, 128), I32),
            pltpu.VMEM((16, 8, 128), I32),
            pltpu.VMEM((4, 128, 512), BF16),
            pltpu.VMEM((4, 128, 128), I32),
            pltpu.VMEM((512, 512), BF16),
            pltpu.VMEM((128, 128), F32),
            pltpu.VMEM((512, 128), BF16),
            pltpu.VMEM((512, 512), BF16),
            pltpu.VMEM((512, 128), F32),
            pltpu.VMEM((256, 128), F32),
            pltpu.VMEM((256, 128), BF16),
            pltpu.VMEM((16, 16, 128), BF16),
            pltpu.VMEM((256, 128), BF16),
            pltpu.VMEM((128, 512), BF16),
            pltpu.VMEM((512, 512), BF16),
            pltpu.VMEM((1, 128), I32),
            pltpu.VMEM((1, 1), I32),
            sem, sem((4,)),
            sem, sem((4, 2)),
            sem((6,)),
            sem, sem((4,)),
            sem, sem((4,)),
            sem, sem((2,)),
            sem, sem,
            sem, sem, sem, sem,
            sem, sem,
            sem, sem,
            sem, sem,
            sem, sem,
            sem, sem,
            sem((1,)),
            pltpu.SemaphoreType.REGULAR((3,)),
        ],
        compiler_params=pltpu.CompilerParams(
            collective_id=0, has_side_effects=True, vmem_limit_bytes=40 * 2**20
        ),
        name="outer_sync",
    )(*[v if v.size == 1 else pltpu.with_memory_space_constraint(v, pltpu.HBM) for v in operands])
    outer, newfb = pl.pallas_call(
        expand,
        out_shape=(jax.ShapeDtypeStruct((512, 512), F32), jax.ShapeDtypeStruct((512, 512), BF16)),
        in_specs=[pl.BlockSpec(memory_space=pltpu.VMEM)] * 3,
        out_specs=(hbm, hbm),
        scratch_shapes=[pltpu.VMEM((512, 512), F32), sem((5,))],
        compiler_params=pltpu.CompilerParams(vmem_limit_bytes=8 * 2**20),
        name="expand_pool",
    )(*[pltpu.with_memory_space_constraint(v, pltpu.VMEM) for v in (res, rank, newfb)])
    return outer, newfb[None]


def solution(mesh):
    placed = (
        P("rep", "shard", None),
        P("rep", "shard", None),
        P("rep", "shard", None),
        P("rep", "shard", None),
        P("rep", "shard"),
        P("rep", "shard", None),
    )
    return jax.shard_map(
        on_device,
        mesh=mesh,
        in_specs=placed,
        out_specs=(P("shard", None), P("rep", "shard", None)),
        check_vma=False,
    )
```
